32 devices in a mesh: grid: 2 (over x), mic: 4 (over z), bin: 4 (over y, core).
Axes of the slice: x: 2, y: 2, z: 4, core: 2. Of those that a mesh axis runs over, the one named last changes fastest.
Arguments:
- grid_points: float32 [3, 2048], P(None, 'grid'), may hold values from -1 to 3, as said below
- mic_coords: float32 [3, 4096], P(None, 'mic'), may hold values from -1 to 1, as said below
- wavenumbers: float32 [16], P('bin'), may hold values from 20 to 150
- pressures: float32 [16, 2, 16, 4096], P('bin', None, None, 'mic'), may hold values from -6 to 6
Outputs:
- solution: float32 [16, 2, 16, 2048], P('bin', None, None, 'grid')
- residual: float32 [16, 2, 16, 4096], P('bin', None, None, 'mic')
The draws below stay inside these ranges and needn't reach their ends.
Inputs may be any that keep to these rules, and one draw needn't show every extreme that they name: `grid_points`: rows 0 and 1 lie in -1 to 1, row 2 in 1 to 3. `mic_coords`: rows 0 and 1 lie in -1 to 1, row 2 in -0.05 to 0.05.
All inputs are finite; a program needn't handle non-finite values.
Results may differ from the reference program's by a relative error of at most 0.0055.
Values may be sent and summed in bfloat16 or wider, within the bound.
A program may use at most 64 MiB of HBM per device.

```python
import math
import jax
import jax.numpy as jnp
from jax import lax

BINS = 16
SNAPS = 16
MICS = 4096
GRID_DEV = 1024
ITERS = 2
GRID = 2048


def draw_grid_points(key, part):
    base = jax.random.uniform(key, (3, GRID), jnp.float32, -1.0, 1.0)
    lift = jnp.array([0.0, 0.0, 2.0], jnp.float32)[:, None]
    return base + lift


def draw_mic_coords(key, part):
    base = jax.random.uniform(key, (3, MICS), jnp.float32, -1.0, 1.0)
    squash = jnp.array([1.0, 1.0, 0.05], jnp.float32)[:, None]
    return base * squash


def shard_levels(rng, dims, pieces, smallest, high):
    def one(position, parts):
        heights = jax.random.uniform(jax.random.fold_in(jax.random.fold_in(rng, 6), position), (parts,), jnp.float32, smallest / len(pieces), high / len(pieces))
        return jnp.repeat(jnp.exp(heights), dims[position] // parts).reshape((-1,) + (1,) * (len(dims) - position - 1))

    factor_of = one(*pieces[0])
    for cut in pieces[1:]:
        factor_of = factor_of * one(*cut)
    return factor_of


def normal_values(stream_key, extent, spread, bound, cuts=(), held_as=jnp.bfloat16):
    drawn = jax.random.normal(stream_key, extent, jnp.float32) * spread
    if len(cuts) > 0:
        drawn = shard_levels(stream_key, extent, cuts, -0.22, 0.18) * drawn
    return jnp.clip(drawn, min=-bound, max=bound).astype(held_as)


def setup_inputs(seed: int = 0) -> dict:
    seeds = jax.random.split(jax.random.key(seed), 5)
    grid_points = draw_grid_points(jax.random.fold_in(seeds[4], 71), 0)
    mic_coords = draw_mic_coords(jax.random.fold_in(seeds[4], 71), 0)
    wavenumbers = jnp.clip(jnp.exp(math.log(150.0) - 2.014903 * jax.random.uniform(seeds[2], (BINS,), jnp.float32) ** shard_levels(seeds[2], (BINS,), ((0, 4),), -0.2, 0.2)), 20.0, 150.0)
    pressures = normal_values(seeds[3], (BINS, 2, SNAPS, MICS), 1.0, 6.0, ((0, 4), (3, 4)), jnp.float32)
    return dict(grid_points=grid_points, mic_coords=mic_coords, wavenumbers=wavenumbers, pressures=pressures)


def steering_tiles(points, mic_coords, wave_number, norm_scale):
    dist_x = points[0][:, None] - mic_coords[0][None, :]
    dist_y = points[1][:, None] - mic_coords[1][None, :]
    dist_z = points[2][:, None] - mic_coords[2][None, :]
    radius = jnp.sqrt(dist_x * dist_x + dist_y * dist_y + dist_z * dist_z)
    amplitude = norm_scale / radius
    phase_angle = wave_number * radius
    cos_tile = (jnp.cos(phase_angle) * amplitude).astype(jnp.bfloat16)
    sin_tile = (jnp.sin(phase_angle) * amplitude).astype(jnp.bfloat16)
    return (cos_tile, sin_tile)

def apply_forward(direction, grid_points, mic_coords, wavenumbers):
    snap_count = direction.shape[2]
    blocks = GRID // GRID_DEV
    rounded = direction.astype(jnp.bfloat16).reshape(BINS, 2 * snap_count, blocks, GRID_DEV).transpose(0, 2, 1, 3)
    point_blocks = grid_points.reshape(3, blocks, GRID_DEV).transpose(1, 0, 2)
    norm_scale = 1.0 / math.sqrt(GRID)

    def one_bin(bin_items):
        wave_number, bin_blocks = bin_items

        def add_block(totals, block_items):
            points, block_piece = block_items
            cos_tile, sin_tile = steering_tiles(points, mic_coords, wave_number, norm_scale)
            cos_sum = totals[0] + jnp.dot(block_piece, cos_tile, preferred_element_type=jnp.float32)
            sin_sum = totals[1] + jnp.dot(block_piece, sin_tile, preferred_element_type=jnp.float32)
            return ((cos_sum, sin_sum), None)
        zero_rows = jnp.zeros((2 * snap_count, MICS), jnp.float32)
        sums, unused = lax.scan(add_block, (zero_rows, zero_rows), (point_blocks, bin_blocks))
        cos_sum, sin_sum = sums
        real_part = cos_sum[:snap_count] + sin_sum[snap_count:]
        imag_part = cos_sum[snap_count:] - sin_sum[:snap_count]
        return jnp.stack([real_part, imag_part])
    return lax.map(one_bin, (wavenumbers, rounded))

def apply_adjoint(residual, grid_points, mic_coords, wavenumbers):
    snap_count = residual.shape[2]
    blocks = GRID // GRID_DEV
    rounded = residual.astype(jnp.bfloat16).reshape(BINS, 2 * snap_count, MICS)
    point_blocks = grid_points.reshape(3, blocks, GRID_DEV).transpose(1, 0, 2)
    norm_scale = 1.0 / math.sqrt(GRID)

    def one_bin(bin_items):
        wave_number, bin_rows = bin_items

        def one_block(points):
            cos_tile, sin_tile = steering_tiles(points, mic_coords, wave_number, norm_scale)
            cos_sum = lax.dot_general(bin_rows, cos_tile, (((1,), (1,)), ((), ())), preferred_element_type=jnp.float32)
            sin_sum = lax.dot_general(bin_rows, sin_tile, (((1,), (1,)), ((), ())), preferred_element_type=jnp.float32)
            real_part = cos_sum[:snap_count] - sin_sum[snap_count:]
            imag_part = cos_sum[snap_count:] + sin_sum[:snap_count]
            return jnp.stack([real_part, imag_part])
        block_images = lax.map(one_block, point_blocks)
        return block_images.transpose(1, 2, 0, 3).reshape(2, snap_count, GRID)
    return lax.map(one_bin, (wavenumbers, rounded))

def reference(grid_points, mic_coords, wavenumbers, pressures):
    residual = pressures
    gradient = apply_adjoint(residual, grid_points, mic_coords, wavenumbers)
    direction = gradient
    grad_norm = jnp.sum(gradient * gradient)
    solution = jnp.zeros_like(gradient)
    for iteration in range(ITERS):
        image = apply_forward(direction, grid_points, mic_coords, wavenumbers)
        image_norm = jnp.sum(image * image)
        step_size = grad_norm / image_norm
        solution = solution + step_size * direction
        residual = residual - step_size * image
        if iteration + 1 < ITERS:
            gradient = apply_adjoint(residual, grid_points, mic_coords, wavenumbers)
            next_norm = jnp.sum(gradient * gradient)
            direction = gradient + next_norm / grad_norm * direction
            grad_norm = next_norm
    return (solution, residual)
```

```python
import functools
import math

import jax
import jax.numpy as jnp
from jax import lax
from jax.experimental import pallas as pl
from jax.experimental.pallas import tpu as pltpu
from jax.sharding import PartitionSpec as P

MESH = pl.DeviceIdType.MESH
F32 = jnp.float32
BF16 = jnp.bfloat16

SIN_COEF = (4.4428679, -7.30744342, 3.59478804, -0.78437393)
COS_COEF = (1.41420408, -6.97764205, 5.71523831, -1.72834838)
ROUNDER = 12582912.0
ROWS = 32
BLOCK = 512


def poly(coef, s):
    total = coef[-1]
    for value in coef[-2::-1]:
        total = total * s + value
    return total


def kernel(norm_scale, gp_ref, mc_ref, wn_ref, p_ref, sol_ref, res_ref,
           gp_all, mc_all, wn_buf, gcol, cos_t, sin_t, p_send, p_all, op_a, op_b,
           part, part_in, grad, image, grad_half, image_half, sol_in, res_in,
           red_out, red_in, red_y, red_y_in,
           co_send, co_recv, p_ssem, p_rsem, ex_ssem, ex_rsem, so_ssem, so_rsem,
           re_ssem, re_rsem, fw_ssem, rd_ssem, rd_rsem, ry_sem):
    x, z, b = lax.axis_index("grid"), lax.axis_index("mic"), lax.axis_index("bin")
    y, c = b // 2, b % 2
    half = z // 2
    n_mic = mc_ref.shape[1]
    n_grid = gp_ref.shape[1]

    def dev(gx, mz, core, plane=None):
        plane = y if plane is None else plane
        return {"grid": gx, "mic": mz, "bin": plane * 2 + core}

    other_core = dev(x, z, 1 - c)

    def rcopy(src, dst, ssem, rsem, device):
        return pltpu.make_async_remote_copy(
            src_ref=src, dst_ref=dst, send_sem=ssem, recv_sem=rsem, device_id=device, device_id_type=MESH)

    offsets = [(dx, dz, dc) for dx in range(2) for dz in range(4) for dc in range(2)][1:]

    def at_offset(o):
        return dev((x + o[0]) % 2, (z + o[1]) % 4, (c + o[2]) % 2)

    barrier = pltpu.get_barrier_semaphore()
    for o in offsets:
        pl.semaphore_signal(barrier, inc=1, device_id=at_offset(o), device_id_type=MESH)
    pl.semaphore_signal(barrier, inc=1, device_id=dev(x, z, c, 1 - y), device_id_type=MESH)
    pl.semaphore_wait(barrier, len(offsets) + 1)

    gp_copy = rcopy(gp_ref, gp_all.at[x], co_send.at[0], co_recv.at[0], dev(1 - x, z, c))
    gp_copy.start()

    def mic_copy(shift):
        return rcopy(mc_ref, mc_all.at[z % 2], co_send.at[1 + shift], co_recv.at[1 + z % 2],
                     dev(x, (z + shift) % 4, c))

    @pl.when(c == half)
    def _():
        for shift in range(1, 4):
            mic_copy(shift).start()
        mc_all[z % 2] = mc_ref[...]

    wn_copy = rcopy(wn_buf, wn_buf, co_send.at[0 + 4], co_recv.at[3], other_core)

    @pl.when(c == x)
    def _():
        wn_buf[...] = jnp.full(wn_buf.shape, wn_ref[z], F32)
        wn_copy.start()

    gp_all[x] = gp_ref[...]

    def p_copy(shift):
        to = (z + shift) % 4
        return rcopy(p_send.at[to], p_all.at[z % 2], p_ssem.at[shift], p_rsem.at[z % 2], dev(x, to, half))

    @pl.when(c == x)
    def _():
        p_send[...] = p_ref[...].astype(BF16)
        for shift in range(4):
            if shift:
                p_copy(shift).start()
            else:
                @pl.when(c != half)
                def _():
                    p_copy(0).start()

                @pl.when(c == half)
                def _():
                    p_all[z % 2] = p_send[z]

    gp_copy.wait_recv()
    for j in range(2):
        @pl.when(z != 2 * c + j)
        def _():
            rcopy(mc_ref, mc_all.at[j], co_send.at[1], co_recv.at[1 + j], other_core).wait_recv()

    @pl.when(c != x)
    def _():
        wn_copy.wait_recv()

    turns = wn_buf[0:1, 0:1] * (1.0 / (2.0 * math.pi))
    amp_scale = turns * norm_scale
    gp_all[...] = gp_all[...] * turns[None]
    mc_all[...] = mc_all[...] * turns[None]
    for h in range(2):
        for d in range(3):
            for k in range(n_grid // 128):
                row = gp_all[h, d:d + 1, k * 128:(k + 1) * 128]
                gcol[d, h * n_grid + k * 128:h * n_grid + (k + 1) * 128, :] = jnp.broadcast_to(row, (128, 128)).T

    scale_row = jnp.broadcast_to(amp_scale, (ROWS, 128))

    @pl.loop(0, 2 * n_grid // ROWS)
    def _(i):
        rows = pl.ds(pl.multiple_of(i * ROWS, ROWS), ROWS)
        gx, gy, gz = gcol[0, rows, :], gcol[1, rows, :], gcol[2, rows, :]
        for j in range(2):
            for k in range(n_mic // 128):
                lanes = slice(k * 128, (k + 1) * 128)
                dx = gx - mc_all[j, 0:1, lanes]
                dy = gy - mc_all[j, 1:2, lanes]
                dz = gz - mc_all[j, 2:3, lanes]
                q = dx * dx + dy * dy + dz * dz
                inv = lax.rsqrt(q)
                t = q * inv
                amp = inv * scale_row
                f = t - ((t + ROUNDER) - ROUNDER)
                s = f * f
                sine = f * poly(SIN_COEF, s)
                cosine = poly(COS_COEF, s)
                scaled = sine * amp
                cols = slice(j * n_mic + k * 128, j * n_mic + (k + 1) * 128)
                cos_t[rows, cols] = (amp - scaled * sine).astype(BF16)
                sin_t[rows, cols] = (scaled * cosine).astype(BF16)

    for j in range(2):
        @pl.when(jnp.logical_not(jnp.logical_and(z == 2 * c + j, c == x)))
        def _():
            rcopy(p_send.at[0], p_all.at[j], p_ssem.at[0], p_rsem.at[j], other_core).wait_recv()

    def operands(blocks, adjoint):
        for j in range(2):
            v = blocks[j]
            real, imag = v[:16], v[16:]
            swapped = [-imag, real] if adjoint else [imag, -real]
            cols = slice(j * v.shape[1], (j + 1) * v.shape[1])
            op_a[:, cols] = v
            op_b[:, cols] = jnp.concatenate(swapped, axis=0)

    def products(accs, pairs):
        out = []
        for acc, (left, right) in zip(accs, pairs):
            prod = left * right
            out.append(acc + jnp.sum(prod.reshape(4, 8, prod.shape[1]), axis=0))
        return out

    def ex_copy(v, k):
        cols = pl.ds(k * BLOCK, BLOCK)
        return rcopy(part.at[v, :, cols], part_in.at[v, :, cols], ex_ssem.at[v, k], ex_rsem.at[v, k], other_core)

    def adjoint(v):
        for k in range(2 * n_grid // BLOCK):
            rows = slice(k * BLOCK, (k + 1) * BLOCK)
            dims = (((1,), (1,)), ((), ()))
            part[v, :, rows] = (
                lax.dot_general(op_a[...], cos_t[rows, :], dims, preferred_element_type=F32)
                + lax.dot_general(op_b[...], sin_t[rows, :], dims, preferred_element_type=F32))
            ex_copy(v, k).start()
        for k in range(2 * n_grid // BLOCK):
            cols = slice(k * BLOCK, (k + 1) * BLOCK)
            ex_copy(v, k).wait_recv()
            total = part[v, :, cols] + part_in[v, :, cols]
            grad[v, :, cols] = total
            h, low = divmod(k * BLOCK, n_grid)
            grad_half[v, h, :, low:low + BLOCK] = total.astype(BF16)

    def forward(v):
        for k in range(2 * n_mic // BLOCK):
            cols = slice(k * BLOCK, (k + 1) * BLOCK)
            total = (jnp.dot(op_a[...], cos_t[:, cols], preferred_element_type=F32)
                     + jnp.dot(op_b[...], sin_t[:, cols], preferred_element_type=F32))
            image[v, :, cols] = total
            h, low = divmod(k * BLOCK, n_mic)
            image_half[v, h, :, low:low + BLOCK] = total.astype(BF16)

    def sol_copy(v, shift):
        to = (z + shift) % 4
        return rcopy(grad_half.at[v, c], sol_in.at[v, z], so_ssem.at[v, shift], so_rsem.at[v, z], dev(c, to, x))

    def send_sol(v):
        for shift in range(1, 4):
            sol_copy(v, shift).start()

        @pl.when(c != x)
        def _():
            sol_copy(v, 0).start()

        @pl.when(c == x)
        def _():
            sol_in[v, z] = grad_half[v, c]

    def res_copy(v, j):
        return rcopy(image_half.at[v, j], res_in.at[v, z], re_ssem.at[v, j], re_rsem.at[v, z], dev(x, 2 * c + j, x))

    def own_quarter(j):
        return jnp.logical_and(z == 2 * c + j, c == x)

    def send_res(v):
        for j in range(2):
            @pl.when(jnp.logical_not(own_quarter(j)))
            def _():
                res_copy(v, j).start()

            @pl.when(own_quarter(j))
            def _():
                res_in[v, z] = image_half[v, j]

    def fw_copy(v, l):
        return rcopy(res_in.at[v, l], res_in.at[v, l], fw_ssem.at[v, l], re_rsem.at[v, l], dev(1 - x, z, c))

    def forward_res(v):
        @pl.when(c == x)
        def _():
            for l in range(4):
                @pl.when(jnp.logical_not(jnp.logical_and(z == l, c == half)))
                def _():
                    fw_copy(v, l).wait_recv()
                fw_copy(v, l).start()

    operands([p_all[0], p_all[1]], True)
    adjoint(0)
    send_sol(0)
    operands([grad_half[0, 0], grad_half[0, 1]], False)
    forward(0)
    send_res(0)
    operands([image_half[0, 0], image_half[0, 1]], True)
    adjoint(1)
    send_sol(1)
    operands([grad_half[1, 0], grad_half[1, 1]], False)
    forward(1)
    send_res(1)
    forward_res(0)

    zero = jnp.zeros((8, 128), F32)
    accs = [zero] * 6
    for k in range(2 * n_grid // 128):
        cols = slice(k * 128, (k + 1) * 128)
        g, u = grad[0, :, cols], grad[1, :, cols]
        accs[:3] = products(accs[:3], [(g, g), (g, u), (u, u)])
    for k in range(2 * n_mic // 128):
        cols = slice(k * 128, (k + 1) * 128)
        q, w = image[0, :, cols], image[1, :, cols]
        accs[3:] = products(accs[3:], [(q, q), (q, w), (w, w)])
    for i in range(6):
        weight = 0.5 if i < 3 else 1.0
        red_out[i:i + 1, :] = weight * jnp.sum(accs[i], axis=0, keepdims=True)
    red_out[6:8, :] = jnp.zeros((2, 128), F32)

    me = (x * 4 + z) * 2 + c

    def rd_copy(i):
        return rcopy(red_out, red_in.at[me], rd_ssem.at[i], rd_rsem.at[i], at_offset(offsets[i]))

    for i in range(len(offsets)):
        rd_copy(i).start()
    red_in[me] = red_out[...]
    for i in range(len(offsets)):
        rd_copy(i).wait_recv()
    total = red_in[0]
    for i in range(1, len(offsets) + 1):
        total = total + red_in[i]
    red_y[...] = total
    y_copy = rcopy(red_y, red_y_in, ry_sem.at[0], ry_sem.at[1], dev(x, z, c, 1 - y))
    y_copy.start()
    forward_res(1)
    y_copy.wait_recv()
    sums = jnp.sum(red_y[...] + red_y_in[...], axis=1, keepdims=True)
    gg, gu, uu, qq, qw, ww = [sums[i:i + 1, :] for i in range(6)]
    step0 = gg / qq
    next_norm = gg - 2.0 * step0 * gu + step0 * step0 * uu
    grown = 1.0 + next_norm / gg
    image_norm = grown * grown * qq - 2.0 * grown * step0 * qw + step0 * step0 * ww
    step1 = next_norm / image_norm
    first = step0 + step1 * grown
    second = -(step1 * step0)

    for l in range(4):
        for v in range(2):
            @pl.when(jnp.logical_not(jnp.logical_and(z == l, c == x)))
            def _():
                rcopy(grad_half.at[v, 0], sol_in.at[v, l], so_ssem.at[v, 0], so_rsem.at[v, l],
                      other_core).wait_recv()
        sol_ref[l] = first * sol_in[0, l].astype(F32) + second * sol_in[1, l].astype(F32)
    for l in range(4):
        @pl.when(c != x)
        def _():
            for v in range(2):
                fw_copy(v, l).wait_recv()
        res_ref[l] = p_ref[l] - (first * res_in[0, l].astype(F32) + second * res_in[1, l].astype(F32))

    gp_copy.wait_send()

    @pl.when(c == half)
    def _():
        for shift in range(1, 4):
            mic_copy(shift).wait_send()

    @pl.when(c == x)
    def _():
        wn_copy.wait_send()
        for shift in range(1, 4):
            p_copy(shift).wait_send()

        @pl.when(c != half)
        def _():
            p_copy(0).wait_send()
        for v in range(2):
            for l in range(4):
                fw_copy(v, l).wait_send()
    for v in range(2):
        for k in range(2 * n_grid // BLOCK):
            ex_copy(v, k).wait_send()
        for shift in range(1, 4):
            sol_copy(v, shift).wait_send()

        @pl.when(c != x)
        def _():
            sol_copy(v, 0).wait_send()
        for j in range(2):
            @pl.when(jnp.logical_not(own_quarter(j)))
            def _():
                res_copy(v, j).wait_send()
    for i in range(len(offsets)):
        rd_copy(i).wait_send()
    y_copy.wait_send()


def per_chip(grid_points, mic_coords, wavenumbers, pressures):
    bins, parts, snaps, mics = pressures.shape
    rows = parts * snaps
    points = grid_points.shape[1]
    norm_scale = 1.0 / math.sqrt(points * lax.axis_size("grid"))
    vmem = pl.BlockSpec(memory_space=pltpu.VMEM)
    dma = pltpu.SemaphoreType.DMA
    blocks = 2 * points // BLOCK
    solution, residual = pl.pallas_call(
        functools.partial(kernel, norm_scale),
        out_shape=(jax.ShapeDtypeStruct((bins, rows, points), F32), jax.ShapeDtypeStruct((bins, rows, mics), F32)),
        in_specs=[vmem, vmem, pl.BlockSpec(memory_space=pltpu.SMEM), vmem],
        out_specs=(vmem, vmem),
        scratch_shapes=[
            pltpu.VMEM((2, 3, points), F32),
            pltpu.VMEM((2, 3, mics), F32),
            pltpu.VMEM((8, 128), F32),
            pltpu.VMEM((3, 2 * points, 128), F32),
            pltpu.VMEM((2 * points, 2 * mics), BF16),
            pltpu.VMEM((2 * points, 2 * mics), BF16),
            pltpu.VMEM((bins, rows, mics), BF16),
            pltpu.VMEM((2, rows, mics), BF16),
            pltpu.VMEM((rows, 2 * mics), BF16),
            pltpu.VMEM((rows, 2 * mics), BF16),
            pltpu.VMEM((2, rows, 2 * points), F32),
            pltpu.VMEM((2, rows, 2 * points), F32),
            pltpu.VMEM((2, rows, 2 * points), F32),
            pltpu.VMEM((2, rows, 2 * mics), F32),
            pltpu.VMEM((2, 2, rows, points), BF16),
            pltpu.VMEM((2, 2, rows, mics), BF16),
            pltpu.VMEM((2, bins, rows, points), BF16),
            pltpu.VMEM((2, bins, rows, mics), BF16),
            pltpu.VMEM((8, 128), F32),
            pltpu.VMEM((16, 8, 128), F32),
            pltpu.VMEM((8, 128), F32),
            pltpu.VMEM((8, 128), F32),
            dma((5,)), dma((4,)), dma((4,)), dma((2,)),
            dma((2, blocks)), dma((2, blocks)), dma((2, 4)), dma((2, 4)),
            dma((2, 2)), dma((2, 4)), dma((2, 4)), dma((15,)), dma((15,)), dma((2,)),
        ],
        compiler_params=pltpu.CompilerParams(
            collective_id=0, has_side_effects=True, vmem_limit_bytes=48 * 1024 * 1024),
    )(grid_points, mic_coords, wavenumbers, pressures.reshape(bins, rows, mics))
    return (solution.reshape(bins, parts, snaps, points), residual.reshape(pressures.shape))


ITERS = 2


def steering_tiles(grid_points, mic_coords, wavenumbers, norm_scale):
    dist_x = grid_points[0][:, None] - mic_coords[0][None, :]
    dist_y = grid_points[1][:, None] - mic_coords[1][None, :]
    dist_z = grid_points[2][:, None] - mic_coords[2][None, :]
    radius = jnp.sqrt(dist_x * dist_x + dist_y * dist_y + dist_z * dist_z)
    amplitude = norm_scale / radius
    cos_list = []
    sin_list = []
    for bin_index in range(wavenumbers.shape[0]):
        phase_angle = wavenumbers[bin_index] * radius
        cos_list.append((jnp.cos(phase_angle) * amplitude).astype(jnp.bfloat16))
        sin_list.append((jnp.sin(phase_angle) * amplitude).astype(jnp.bfloat16))
    return (jnp.stack(cos_list), jnp.stack(sin_list))


def body(grid_points, mic_coords, wavenumbers, pressures):
    bin_count = pressures.shape[0]
    snap_count = pressures.shape[2]
    grid_local = grid_points.shape[1]
    norm_scale = 1.0 / math.sqrt(grid_local * lax.axis_size("grid"))
    cos_tiles, sin_tiles = steering_tiles(grid_points, mic_coords, wavenumbers, norm_scale)

    def combine_adjoint(cos_sum, sin_sum):
        real_part = cos_sum[:, :snap_count] - sin_sum[:, snap_count:]
        imag_part = cos_sum[:, snap_count:] + sin_sum[:, :snap_count]
        return jnp.stack([real_part, imag_part], axis=1)

    def apply_adjoint(residual):
        rounded = residual.astype(jnp.bfloat16).reshape(
            bin_count, 2 * snap_count, residual.shape[3]
        )
        cos_sum = jnp.einsum("fkm,fgm->fkg", rounded, cos_tiles, preferred_element_type=jnp.float32)
        sin_sum = jnp.einsum("fkm,fgm->fkg", rounded, sin_tiles, preferred_element_type=jnp.float32)
        partial_terms = combine_adjoint(cos_sum, sin_sum)
        summed = lax.psum(partial_terms, "mic")
        grad_norm = lax.psum(jnp.sum(summed * summed), ("grid", "bin"))
        return (summed, grad_norm)

    residual = pressures
    gradient, grad_norm = apply_adjoint(residual)
    direction = gradient
    solution = jnp.zeros_like(gradient)
    for iteration in range(ITERS):
        apply_rounded = direction.astype(jnp.bfloat16).reshape(
            bin_count, 2 * snap_count, direction.shape[3]
        )
        apply_cos_sum = jnp.einsum(
            "fkg,fgm->fkm", apply_rounded, cos_tiles, preferred_element_type=jnp.float32
        )
        apply_sin_sum = jnp.einsum(
            "fkg,fgm->fkm", apply_rounded, sin_tiles, preferred_element_type=jnp.float32
        )
        combine_real_part = apply_cos_sum[:, :snap_count] + apply_sin_sum[:, snap_count:]
        combine_imag_part = apply_cos_sum[:, snap_count:] - apply_sin_sum[:, :snap_count]
        apply_partial_terms = jnp.stack([combine_real_part, combine_imag_part], axis=1)
        apply_summed = lax.psum(apply_partial_terms, "grid")
        image_norm = lax.psum(jnp.sum(apply_summed * apply_summed), ("mic", "bin"))
        image, image_norm = (apply_summed, image_norm)
        step_size = grad_norm / image_norm
        solution = solution + step_size * direction
        residual = residual - step_size * image
        if iteration + 1 < ITERS:
            gradient, next_norm = apply_adjoint(residual)
            direction = gradient + next_norm / grad_norm * direction
            grad_norm = next_norm
    return (solution, residual)


def solution(mesh):
    placed = (P(None, "grid"), P(None, "mic"), P("bin"), P("bin", None, None, "mic"))
    sizes = (mesh.shape["grid"], mesh.shape["mic"], mesh.shape["bin"])
    return jax.shard_map(
        per_chip if sizes == (2, 4, 4) else body,
        mesh=mesh,
        in_specs=placed,
        out_specs=(P("bin", None, None, "grid"), P("bin", None, None, "mic")),
        check_vma=False,
    )
```

```python
import functools
import math

import jax
import jax.numpy as jnp
from jax import lax
from jax.experimental import pallas as pl
from jax.experimental.pallas import tpu as pltpu
from jax.sharding import PartitionSpec as P

MESH = pl.DeviceIdType.MESH
F32 = jnp.float32
BF16 = jnp.bfloat16

SIN_COEF = (4.4428679, -7.30744342, 3.59478804, -0.78437393)
COS_COEF = (1.41420408, -6.97764205, 5.71523831, -1.72834838)
ROUNDER = 12582912.0
ROWS = 64
TILE = 256
BLOCK = 512


def poly(coef, s):
    total = coef[-1]
    for value in coef[-2::-1]:
        total = total * s + value
    return total


def kernel(norm_scale, gp_ref, mc_ref, wn_ref, p_ref, sol_ref, res_ref,
           gp_all, mc_all, wn_buf, p_loc, g_rows, m_rows, g_mat, m_mat, cos_t, sin_t, p_send, p_all, op_a, op_b,
           part, part_in, grad, image, grad_half, image_half, sol_in, res_in,
           red_out, red_in, red_y, red_y_in,
           co_send, co_recv, p_ssem, p_rsem, ex_ssem, ex_rsem, so_ssem, so_rsem,
           re_ssem, re_rsem, fw_ssem, rd_ssem, rd_rsem, ry_sem, in_sem):
    x, z, b = lax.axis_index("grid"), lax.axis_index("mic"), lax.axis_index("bin")
    y, c = b // 2, b % 2
    half = z // 2
    n_mic = mc_ref.shape[1]
    n_grid = gp_ref.shape[1]

    def dev(gx, mz, core, plane=None):
        plane = y if plane is None else plane
        return {"grid": gx, "mic": mz, "bin": plane * 2 + core}

    other_core = dev(x, z, 1 - c)

    def rcopy(src, dst, ssem, rsem, device):
        return pltpu.make_async_remote_copy(
            src_ref=src, dst_ref=dst, send_sem=ssem, recv_sem=rsem, device_id=device, device_id_type=MESH)

    offsets = [(dx, dz, dc) for dx in range(2) for dz in range(4) for dc in range(2)][1:]

    def at_offset(o):
        return dev((x + o[0]) % 2, (z + o[1]) % 4, (c + o[2]) % 2)

    barrier = pltpu.get_barrier_semaphore()
    for o in offsets:
        pl.semaphore_signal(barrier, inc=1, device_id=at_offset(o), device_id_type=MESH)
    pl.semaphore_signal(barrier, inc=1, device_id=dev(x, z, c, 1 - y), device_id_type=MESH)
    p_load = pltpu.make_async_copy(p_ref, p_loc, in_sem.at[0])
    p_load.start()
    gp_load = pltpu.make_async_copy(gp_ref, gp_all.at[x], in_sem.at[1])
    gp_load.start()
    mc_load = pltpu.make_async_copy(mc_ref, mc_all.at[z % 2], in_sem.at[2])
    wn_load = pltpu.make_async_copy(wn_ref, wn_buf, in_sem.at[3])

    @pl.when(c == half)
    def _():
        mc_load.start()

    @pl.when(c == x)
    def _():
        wn_load.start()

    g_rows[...] = jnp.zeros(g_rows.shape, F32)
    m_rows[...] = jnp.zeros(m_rows.shape, F32)
    m_mat[...] = jnp.zeros(m_mat.shape, BF16)
    pl.semaphore_wait(barrier, len(offsets) + 1)

    gp_copy = rcopy(gp_ref, gp_all.at[x], co_send.at[0], co_recv.at[0], dev(1 - x, z, c))
    gp_copy.start()

    def mic_copy(shift):
        return rcopy(mc_ref, mc_all.at[z % 2], co_send.at[1 + shift], co_recv.at[1 + z % 2],
                     dev(x, (z + shift) % 4, c))

    @pl.when(c == half)
    def _():
        for shift in range(1, 4):
            mic_copy(shift).start()

    wn_copy = rcopy(wn_ref, wn_buf, co_send.at[0 + 4], co_recv.at[3], other_core)

    @pl.when(c == x)
    def _():
        wn_copy.start()

    def p_copy(shift):
        to = (z + shift) % 4
        return rcopy(p_send.at[to], p_all.at[z % 2], p_ssem.at[shift], p_rsem.at[z % 2], dev(x, to, half))

    p_load.wait()

    @pl.when(c == x)
    def _():
        p_send[...] = p_loc[...].astype(BF16)
        for shift in range(4):
            if shift:
                p_copy(shift).start()
            else:
                @pl.when(c != half)
                def _():
                    p_copy(0).start()

                @pl.when(c == half)
                def _():
                    p_all[z % 2] = p_send[z]

    gp_load.wait()

    @pl.when(c == half)
    def _():
        mc_load.wait()

    @pl.when(c == x)
    def _():
        wn_load.wait()

    gp_copy.wait_recv()
    for j in range(2):
        @pl.when(z != 2 * c + j)
        def _():
            rcopy(mc_ref, mc_all.at[j], co_send.at[1], co_recv.at[1 + j], other_core).wait_recv()

    @pl.when(c != x)
    def _():
        wn_copy.wait_recv()

    here = lax.broadcasted_iota(jnp.int32, wn_buf.shape, 1) == z
    wavenumber = jnp.sum(jnp.where(here, wn_buf[...], 0.0), axis=1, keepdims=True)
    turns = wavenumber * (1.0 / (2.0 * math.pi))
    scale_row = jnp.broadcast_to(turns * norm_scale, (32, 128))

    def pieces(v):
        high = v.astype(BF16).astype(F32)
        rest = v - high
        mid = rest.astype(BF16).astype(F32)
        return high, mid, (rest - mid).astype(BF16).astype(F32)

    def fill(out, h, width, left, norm_at, one_at, v):
        cols = slice(h * width, (h + 1) * width)
        split = pieces(v)
        for i, which in enumerate(left):
            out[3 * i:3 * i + 3, cols] = split[which]
        for i, value in enumerate(pieces(jnp.sum(v * v, axis=0, keepdims=True))):
            out[norm_at + i:norm_at + i + 1, cols] = value
        out[one_at:one_at + 3, cols] = jnp.ones((3, width), F32)

    for h in range(2):
        fill(g_rows, h, n_grid, (0, 0, 1, 1, 0, 2), 18, 21, gp_all[h] * turns)
        fill(m_rows, h, n_mic, (0, 1, 0, 1, 2, 0), 21, 18, mc_all[h] * turns)
    row_index = lax.broadcasted_iota(jnp.int32, (32, 1), 0)
    m_mat[0:32, :] = (m_rows[...] * jnp.where(row_index < 18, -2.0, 1.0)).astype(BF16)
    for k in range(2 * n_grid // 128):
        g_mat[k * 128:(k + 1) * 128, :] = g_rows[:, k * 128:(k + 1) * 128].T.astype(BF16)

    @pl.loop(0, 2 * n_grid // ROWS)
    def _(i):
        base = pl.multiple_of(i * ROWS, ROWS)
        points = g_mat[pl.ds(base, ROWS), :]
        for n in range(2 * n_mic // TILE):
            squares = jnp.dot(points, m_mat[:, n * TILE:(n + 1) * TILE], preferred_element_type=F32)
            for r in range(ROWS // 32):
                for k in range(TILE // 128):
                    q = squares[r * 32:(r + 1) * 32, k * 128:(k + 1) * 128]
                    inv = lax.rsqrt(q)
                    t = q * inv
                    amp = inv * scale_row
                    f = t - ((t + ROUNDER) - ROUNDER)
                    s = f * f
                    sine = f * poly(SIN_COEF, s)
                    cosine = poly(COS_COEF, s)
                    scaled = sine * amp
                    rows = pl.ds(base + r * 32, 32)
                    cols = slice(n * TILE + k * 128, n * TILE + (k + 1) * 128)
                    cos_t[rows, cols] = (amp - scaled * sine).astype(BF16)
                    sin_t[rows, cols] = (scaled * cosine).astype(BF16)

    for j in range(2):
        @pl.when(jnp.logical_not(jnp.logical_and(z == 2 * c + j, c == x)))
        def _():
            rcopy(p_send.at[0], p_all.at[j], p_ssem.at[0], p_rsem.at[j], other_core).wait_recv()

    def operands(blocks, adjoint):
        for j in range(2):
            v = blocks[j]
            real, imag = v[:16], v[16:]
            swapped = [-imag, real] if adjoint else [imag, -real]
            cols = slice(j * v.shape[1], (j + 1) * v.shape[1])
            op_a[:, cols] = v
            op_b[:, cols] = jnp.concatenate(swapped, axis=0)

    def products(accs, pairs):
        out = []
        for acc, (left, right) in zip(accs, pairs):
            prod = left * right
            out.append(acc + jnp.sum(prod.reshape(4, 8, prod.shape[1]), axis=0))
        return out

    def ex_copy(v, k):
        cols = pl.ds(k * BLOCK, BLOCK)
        return rcopy(part.at[v, :, cols], part_in.at[v, :, cols], ex_ssem.at[v, k], ex_rsem.at[v, k], other_core)

    def adjoint(v):
        for k in range(2 * n_grid // BLOCK):
            rows = slice(k * BLOCK, (k + 1) * BLOCK)
            dims = (((1,), (1,)), ((), ()))
            part[v, :, rows] = (
                lax.dot_general(op_a[...], cos_t[rows, :], dims, preferred_element_type=F32)
                + lax.dot_general(op_b[...], sin_t[rows, :], dims, preferred_element_type=F32))
            ex_copy(v, k).start()
        for k in range(2 * n_grid // BLOCK):
            cols = slice(k * BLOCK, (k + 1) * BLOCK)
            ex_copy(v, k).wait_recv()
            total = part[v, :, cols] + part_in[v, :, cols]
            grad[v, :, cols] = total
            h, low = divmod(k * BLOCK, n_grid)
            grad_half[v, h, :, low:low + BLOCK] = total.astype(BF16)

    def forward(v):
        for k in range(2 * n_mic // BLOCK):
            cols = slice(k * BLOCK, (k + 1) * BLOCK)
            total = (jnp.dot(op_a[...], cos_t[:, cols], preferred_element_type=F32)
                     + jnp.dot(op_b[...], sin_t[:, cols], preferred_element_type=F32))
            image[v, :, cols] = total
            h, low = divmod(k * BLOCK, n_mic)
            image_half[v, h, :, low:low + BLOCK] = total.astype(BF16)

    def sol_copy(v, shift):
        to = (z + shift) % 4
        return rcopy(grad_half.at[v, c], sol_in.at[v, z], so_ssem.at[v, shift], so_rsem.at[v, z], dev(c, to, x))

    def send_sol(v):
        for shift in range(1, 4):
            sol_copy(v, shift).start()

        @pl.when(c != x)
        def _():
            sol_copy(v, 0).start()

        @pl.when(c == x)
        def _():
            sol_in[v, z] = grad_half[v, c]

    def res_copy(v, j):
        return rcopy(image_half.at[v, j], res_in.at[v, z], re_ssem.at[v, j], re_rsem.at[v, z], dev(x, 2 * c + j, x))

    def own_quarter(j):
        return jnp.logical_and(z == 2 * c + j, c == x)

    def send_res(v):
        for j in range(2):
            @pl.when(jnp.logical_not(own_quarter(j)))
            def _():
                res_copy(v, j).start()

            @pl.when(own_quarter(j))
            def _():
                res_in[v, z] = image_half[v, j]

    def fw_copy(v, l):
        return rcopy(res_in.at[v, l], res_in.at[v, l], fw_ssem.at[v, l], re_rsem.at[v, l], dev(1 - x, z, c))

    def forward_res(v):
        @pl.when(c == x)
        def _():
            for l in range(4):
                @pl.when(jnp.logical_not(jnp.logical_and(z == l, c == half)))
                def _():
                    fw_copy(v, l).wait_recv()
                fw_copy(v, l).start()

    operands([p_all[0], p_all[1]], True)
    adjoint(0)
    send_sol(0)
    operands([grad_half[0, 0], grad_half[0, 1]], False)
    forward(0)
    send_res(0)
    operands([image_half[0, 0], image_half[0, 1]], True)
    adjoint(1)
    send_sol(1)
    operands([grad_half[1, 0], grad_half[1, 1]], False)
    forward(1)
    send_res(1)
    forward_res(0)

    zero = jnp.zeros((8, 128), F32)
    accs = [zero] * 6
    for k in range(2 * n_grid // 128):
        cols = slice(k * 128, (k + 1) * 128)
        g, u = grad[0, :, cols], grad[1, :, cols]
        accs[:3] = products(accs[:3], [(g, g), (g, u), (u, u)])
    for k in range(2 * n_mic // 128):
        cols = slice(k * 128, (k + 1) * 128)
        q, w = image[0, :, cols], image[1, :, cols]
        accs[3:] = products(accs[3:], [(q, q), (q, w), (w, w)])
    for i in range(6):
        weight = 0.5 if i < 3 else 1.0
        red_out[i:i + 1, :] = weight * jnp.sum(accs[i], axis=0, keepdims=True)
    red_out[6:8, :] = jnp.zeros((2, 128), F32)

    me = (x * 4 + z) * 2 + c

    def rd_copy(i):
        return rcopy(red_out, red_in.at[me], rd_ssem.at[i], rd_rsem.at[i], at_offset(offsets[i]))

    for i in range(len(offsets)):
        rd_copy(i).start()
    red_in[me] = red_out[...]
    for i in range(len(offsets)):
        rd_copy(i).wait_recv()
    total = red_in[0]
    for i in range(1, len(offsets) + 1):
        total = total + red_in[i]
    red_y[...] = total
    y_copy = rcopy(red_y, red_y_in, ry_sem.at[0], ry_sem.at[1], dev(x, z, c, 1 - y))
    y_copy.start()
    forward_res(1)
    y_copy.wait_recv()
    sums = jnp.sum(red_y[...] + red_y_in[...], axis=1, keepdims=True)
    gg, gu, uu, qq, qw, ww = [sums[i:i + 1, :] for i in range(6)]
    step0 = gg / qq
    next_norm = gg - 2.0 * step0 * gu + step0 * step0 * uu
    grown = 1.0 + next_norm / gg
    image_norm = grown * grown * qq - 2.0 * grown * step0 * qw + step0 * step0 * ww
    step1 = next_norm / image_norm
    first = step0 + step1 * grown
    second = -(step1 * step0)

    for l in range(4):
        for v in range(2):
            @pl.when(jnp.logical_not(jnp.logical_and(z == l, c == x)))
            def _():
                rcopy(grad_half.at[v, 0], sol_in.at[v, l], so_ssem.at[v, 0], so_rsem.at[v, l],
                      other_core).wait_recv()
        sol_ref[l] = first * sol_in[0, l].astype(F32) + second * sol_in[1, l].astype(F32)
    for l in range(4):
        @pl.when(c != x)
        def _():
            for v in range(2):
                fw_copy(v, l).wait_recv()
        res_ref[l] = p_loc[l] - (first * res_in[0, l].astype(F32) + second * res_in[1, l].astype(F32))

    gp_copy.wait_send()

    @pl.when(c == half)
    def _():
        for shift in range(1, 4):
            mic_copy(shift).wait_send()

    @pl.when(c == x)
    def _():
        wn_copy.wait_send()
        for shift in range(1, 4):
            p_copy(shift).wait_send()

        @pl.when(c != half)
        def _():
            p_copy(0).wait_send()
        for v in range(2):
            for l in range(4):
                fw_copy(v, l).wait_send()
    for v in range(2):
        for k in range(2 * n_grid // BLOCK):
            ex_copy(v, k).wait_send()
        for shift in range(1, 4):
            sol_copy(v, shift).wait_send()

        @pl.when(c != x)
        def _():
            sol_copy(v, 0).wait_send()
        for j in range(2):
            @pl.when(jnp.logical_not(own_quarter(j)))
            def _():
                res_copy(v, j).wait_send()
    for i in range(len(offsets)):
        rd_copy(i).wait_send()
    y_copy.wait_send()


def per_chip(grid_points, mic_coords, wavenumbers, pressures):
    bins, parts, snaps, mics = pressures.shape
    rows = parts * snaps
    points = grid_points.shape[1]
    norm_scale = 1.0 / math.sqrt(points * lax.axis_size("grid"))
    vmem = pl.BlockSpec(memory_space=pltpu.VMEM)
    dma = pltpu.SemaphoreType.DMA
    blocks = 2 * points // BLOCK
    solution, residual = pl.pallas_call(
        functools.partial(kernel, norm_scale),
        out_shape=(jax.ShapeDtypeStruct((bins, rows, points), F32), jax.ShapeDtypeStruct((bins, rows, mics), F32)),
        in_specs=[pl.BlockSpec(memory_space=pltpu.HBM)] * 4,
        out_specs=(vmem, vmem),
        scratch_shapes=[
            pltpu.VMEM((2, 3, points), F32),
            pltpu.VMEM((2, 3, mics), F32),
            pltpu.VMEM((1, bins), F32),
            pltpu.VMEM((bins, rows, mics), F32),
            pltpu.VMEM((128, 2 * points), F32),
            pltpu.VMEM((32, 2 * mics), F32),
            pltpu.VMEM((2 * points, 128), BF16),
            pltpu.VMEM((128, 2 * mics), BF16),
            pltpu.VMEM((2 * points, 2 * mics), BF16),
            pltpu.VMEM((2 * points, 2 * mics), BF16),
            pltpu.VMEM((bins, rows, mics), BF16),
            pltpu.VMEM((2, rows, mics), BF16),
            pltpu.VMEM((rows, 2 * mics), BF16),
            pltpu.VMEM((rows, 2 * mics), BF16),
            pltpu.VMEM((2, rows, 2 * points), F32),
            pltpu.VMEM((2, rows, 2 * points), F32),
            pltpu.VMEM((2, rows, 2 * points), F32),
            pltpu.VMEM((2, rows, 2 * mics), F32),
            pltpu.VMEM((2, 2, rows, points), BF16),
            pltpu.VMEM((2, 2, rows, mics), BF16),
            pltpu.VMEM((2, bins, rows, points), BF16),
            pltpu.VMEM((2, bins, rows, mics), BF16),
            pltpu.VMEM((8, 128), F32),
            pltpu.VMEM((16, 8, 128), F32),
            pltpu.VMEM((8, 128), F32),
            pltpu.VMEM((8, 128), F32),
            dma((5,)), dma((4,)), dma((4,)), dma((2,)),
            dma((2, blocks)), dma((2, blocks)), dma((2, 4)), dma((2, 4)),
            dma((2, 2)), dma((2, 4)), dma((2, 4)), dma((15,)), dma((15,)), dma((2,)), dma((4,)),
        ],
        compiler_params=pltpu.CompilerParams(
            collective_id=0, has_side_effects=True, vmem_limit_bytes=48 * 1024 * 1024),
    )(grid_points, mic_coords, wavenumbers.reshape(1, bins), pressures.reshape(bins, rows, mics))
    return (solution.reshape(bins, parts, snaps, points), residual.reshape(pressures.shape))


ITERS = 2


def steering_tiles(grid_points, mic_coords, wavenumbers, norm_scale):
    dist_x = grid_points[0][:, None] - mic_coords[0][None, :]
    dist_y = grid_points[1][:, None] - mic_coords[1][None, :]
    dist_z = grid_points[2][:, None] - mic_coords[2][None, :]
    radius = jnp.sqrt(dist_x * dist_x + dist_y * dist_y + dist_z * dist_z)
    amplitude = norm_scale / radius
    cos_list = []
    sin_list = []
    for bin_index in range(wavenumbers.shape[0]):
        phase_angle = wavenumbers[bin_index] * radius
        cos_list.append((jnp.cos(phase_angle) * amplitude).astype(jnp.bfloat16))
        sin_list.append((jnp.sin(phase_angle) * amplitude).astype(jnp.bfloat16))
    return (jnp.stack(cos_list), jnp.stack(sin_list))


def body(grid_points, mic_coords, wavenumbers, pressures):
    bin_count = pressures.shape[0]
    snap_count = pressures.shape[2]
    grid_local = grid_points.shape[1]
    norm_scale = 1.0 / math.sqrt(grid_local * lax.axis_size("grid"))
    cos_tiles, sin_tiles = steering_tiles(grid_points, mic_coords, wavenumbers, norm_scale)

    def combine_adjoint(cos_sum, sin_sum):
        real_part = cos_sum[:, :snap_count] - sin_sum[:, snap_count:]
        imag_part = cos_sum[:, snap_count:] + sin_sum[:, :snap_count]
        return jnp.stack([real_part, imag_part], axis=1)

    def apply_adjoint(residual):
        rounded = residual.astype(jnp.bfloat16).reshape(
            bin_count, 2 * snap_count, residual.shape[3]
        )
        cos_sum = jnp.einsum("fkm,fgm->fkg", rounded, cos_tiles, preferred_element_type=jnp.float32)
        sin_sum = jnp.einsum("fkm,fgm->fkg", rounded, sin_tiles, preferred_element_type=jnp.float32)
        partial_terms = combine_adjoint(cos_sum, sin_sum)
        summed = lax.psum(partial_terms, "mic")
        grad_norm = lax.psum(jnp.sum(summed * summed), ("grid", "bin"))
        return (summed, grad_norm)

    residual = pressures
    gradient, grad_norm = apply_adjoint(residual)
    direction = gradient
    solution = jnp.zeros_like(gradient)
    for iteration in range(ITERS):
        apply_rounded = direction.astype(jnp.bfloat16).reshape(
            bin_count, 2 * snap_count, direction.shape[3]
        )
        apply_cos_sum = jnp.einsum(
            "fkg,fgm->fkm", apply_rounded, cos_tiles, preferred_element_type=jnp.float32
        )
        apply_sin_sum = jnp.einsum(
            "fkg,fgm->fkm", apply_rounded, sin_tiles, preferred_element_type=jnp.float32
        )
        combine_real_part = apply_cos_sum[:, :snap_count] + apply_sin_sum[:, snap_count:]
        combine_imag_part = apply_cos_sum[:, snap_count:] - apply_sin_sum[:, :snap_count]
        apply_partial_terms = jnp.stack([combine_real_part, combine_imag_part], axis=1)
        apply_summed = lax.psum(apply_partial_terms, "grid")
        image_norm = lax.psum(jnp.sum(apply_summed * apply_summed), ("mic", "bin"))
        image, image_norm = (apply_summed, image_norm)
        step_size = grad_norm / image_norm
        solution = solution + step_size * direction
        residual = residual - step_size * image
        if iteration + 1 < ITERS:
            gradient, next_norm = apply_adjoint(residual)
            direction = gradient + next_norm / grad_norm * direction
            grad_norm = next_norm
    return (solution, residual)


def solution(mesh):
    placed = (P(None, "grid"), P(None, "mic"), P("bin"), P("bin", None, None, "mic"))
    sizes = (mesh.shape["grid"], mesh.shape["mic"], mesh.shape["bin"])
    return jax.shard_map(
        per_chip if sizes == (2, 4, 4) else body,
        mesh=mesh,
        in_specs=placed,
        out_specs=(P("bin", None, None, "grid"), P("bin", None, None, "mic")),
        check_vma=False,
    )
```

```python
import functools
import math

import jax
import jax.numpy as jnp
from jax import lax
from jax.experimental import pallas as pl
from jax.experimental.pallas import tpu as pltpu
from jax.sharding import PartitionSpec as P

MESH = pl.DeviceIdType.MESH
F32 = jnp.float32
BF16 = jnp.bfloat16

SIN_COEF = (4.4428679, -7.30744342, 3.59478804, -0.78437393)
COS_COEF = (1.41420408, -6.97764205, 5.71523831, -1.72834838)
ROUNDER = 12582912.0
ROWS = 64
TILE = 256
BLOCK = 512


def poly(coef, s):
    total = coef[-1]
    for value in coef[-2::-1]:
        total = total * s + value
    return total


def kernel(norm_scale, gp_ref, mc_ref, wn_ref, p_ref, sol_ref, res_ref,
           gp_all, mc_all, wn_buf, p_loc, g_rows, m_rows, g_mat, m_mat, sq_even, sq_odd, cos_t, sin_t, p_send, p_all, op_a, op_b, col_a, col_b,
           part, part_in, grad, image, grad_half, image_half, sol_in, res_in,
           red_out, red_in, red_y, red_y_in,
           co_send, co_recv, p_ssem, p_rsem, ex_ssem, ex_rsem, so_ssem, so_rsem,
           re_ssem, re_rsem, fw_ssem, rd_ssem, rd_rsem, ry_sem, in_sem, rl_ssem):
    x, z, b = lax.axis_index("grid"), lax.axis_index("mic"), lax.axis_index("bin")
    y, c = b // 2, b % 2
    half = z // 2
    n_mic = mc_ref.shape[1]
    n_grid = gp_ref.shape[1]

    def dev(gx, mz, core, plane=None):
        plane = y if plane is None else plane
        return {"grid": gx, "mic": mz, "bin": plane * 2 + core}

    other_core = dev(x, z, 1 - c)

    def rcopy(src, dst, ssem, rsem, device):
        return pltpu.make_async_remote_copy(
            src_ref=src, dst_ref=dst, send_sem=ssem, recv_sem=rsem, device_id=device, device_id_type=MESH)

    offsets = [(dx, dz, dc) for dx in range(2) for dz in range(4) for dc in range(2)][1:]

    def at_offset(o):
        return dev((x + o[0]) % 2, (z + o[1]) % 4, (c + o[2]) % 2)

    barrier = pltpu.get_barrier_semaphore()
    for o in offsets:
        pl.semaphore_signal(barrier, inc=1, device_id=at_offset(o), device_id_type=MESH)
    pl.semaphore_signal(barrier, inc=1, device_id=dev(x, z, c, 1 - y), device_id_type=MESH)
    p_load = pltpu.make_async_copy(p_ref, p_loc, in_sem.at[0])
    p_load.start()
    gp_load = pltpu.make_async_copy(gp_ref, gp_all.at[x], in_sem.at[1])
    gp_load.start()
    mc_load = pltpu.make_async_copy(mc_ref, mc_all.at[z % 2], in_sem.at[2])
    wn_load = pltpu.make_async_copy(wn_ref, wn_buf, in_sem.at[3])

    @pl.when(c == half)
    def _():
        mc_load.start()

    @pl.when(c == x)
    def _():
        wn_load.start()

    g_rows[...] = jnp.zeros(g_rows.shape, F32)
    m_rows[...] = jnp.zeros(m_rows.shape, F32)
    m_mat[...] = jnp.zeros(m_mat.shape, BF16)
    pl.semaphore_wait(barrier, len(offsets) + 1)

    gp_copy = rcopy(gp_ref, gp_all.at[x], co_send.at[0], co_recv.at[0], dev(1 - x, z, c))
    gp_copy.start()

    def mic_copy(shift):
        return rcopy(mc_ref, mc_all.at[z % 2], co_send.at[1 + shift], co_recv.at[1 + z % 2],
                     dev(x, (z + shift) % 4, c))

    @pl.when(c == half)
    def _():
        for shift in range(1, 4):
            mic_copy(shift).start()

    wn_copy = rcopy(wn_ref, wn_buf, co_send.at[0 + 4], co_recv.at[3], other_core)

    @pl.when(c == x)
    def _():
        wn_copy.start()

    def p_copy(shift):
        to = (z + shift) % 4
        return rcopy(p_send.at[to], p_all.at[z % 2], p_ssem.at[shift], p_rsem.at[z % 2], dev(x, to, half))

    p_load.wait()

    @pl.when(c == x)
    def _():
        p_send[...] = p_loc[...].astype(BF16)
        for shift in range(4):
            if shift:
                p_copy(shift).start()
            else:
                @pl.when(c != half)
                def _():
                    p_copy(0).start()

                @pl.when(c == half)
                def _():
                    p_all[z % 2] = p_send[z]

    gp_load.wait()

    @pl.when(c == half)
    def _():
        mc_load.wait()

    @pl.when(c == x)
    def _():
        wn_load.wait()

    gp_copy.wait_recv()
    for j in range(2):
        @pl.when(z != 2 * c + j)
        def _():
            rcopy(mc_ref, mc_all.at[j], co_send.at[1], co_recv.at[1 + j], other_core).wait_recv()

    @pl.when(c != x)
    def _():
        wn_copy.wait_recv()

    here = lax.broadcasted_iota(jnp.int32, wn_buf.shape, 1) == z
    wavenumber = jnp.sum(jnp.where(here, wn_buf[...], 0.0), axis=1, keepdims=True)
    turns = wavenumber * (1.0 / (2.0 * math.pi))
    scale_row = jnp.broadcast_to(turns * norm_scale, (32, 128))

    def pieces(v):
        high = v.astype(BF16).astype(F32)
        rest = v - high
        mid = rest.astype(BF16).astype(F32)
        return high, mid, (rest - mid).astype(BF16).astype(F32)

    def fill(out, h, width, left, norm_at, one_at, v):
        cols = slice(h * width, (h + 1) * width)
        split = pieces(v)
        for i, which in enumerate(left):
            out[3 * i:3 * i + 3, cols] = split[which]
        for i, value in enumerate(pieces(jnp.sum(v * v, axis=0, keepdims=True))):
            out[norm_at + i:norm_at + i + 1, cols] = value
        out[one_at:one_at + 3, cols] = jnp.ones((3, width), F32)

    for h in range(2):
        fill(g_rows, h, n_grid, (0, 0, 1, 1, 0, 2), 18, 21, gp_all[h] * turns)
        fill(m_rows, h, n_mic, (0, 1, 0, 1, 2, 0), 21, 18, mc_all[h] * turns)
    row_index = lax.broadcasted_iota(jnp.int32, (32, 1), 0)
    m_mat[0:32, :] = (m_rows[...] * jnp.where(row_index < 18, -2.0, 1.0)).astype(BF16)
    for k in range(2 * n_grid // 128):
        g_mat[k * 128:(k + 1) * 128, :] = g_rows[:, k * 128:(k + 1) * 128].T.astype(BF16)

    def squares(i, out):
        points = g_mat[pl.ds(pl.multiple_of(i * ROWS, ROWS), ROWS), :]
        for n in range(2 * n_mic // TILE):
            cols = slice(n * TILE, (n + 1) * TILE)
            out[:, cols] = jnp.dot(points, m_mat[:, cols], preferred_element_type=F32)

    def tiles(i, source):
        base = pl.multiple_of(i * ROWS, ROWS)
        for k in range(2 * n_mic // 128):
            cols = slice(k * 128, (k + 1) * 128)
            for r in range(0, ROWS, 32):
                q = source[r:r + 32, cols]
                inv = lax.rsqrt(q)
                t = q * inv
                amp = inv * scale_row
                f = t - ((t + ROUNDER) - ROUNDER)
                s = f * f
                sine = f * poly(SIN_COEF, s)
                cosine = poly(COS_COEF, s)
                scaled = sine * amp
                rows = pl.ds(base + r, 32)
                cos_t[rows, cols] = (amp - scaled * sine).astype(BF16)
                sin_t[rows, cols] = (scaled * cosine).astype(BF16)

    steps = 2 * n_grid // ROWS
    squares(0, sq_even)

    @pl.loop(0, steps // 2)
    def _(i):
        squares(2 * i + 1, sq_odd)
        tiles(2 * i, sq_even)
        squares(jnp.minimum(2 * i + 2, steps - 1), sq_even)
        tiles(2 * i + 1, sq_odd)

    for j in range(2):
        @pl.when(jnp.logical_not(jnp.logical_and(z == 2 * c + j, c == x)))
        def _():
            rcopy(p_send.at[0], p_all.at[j], p_ssem.at[0], p_rsem.at[j], other_core).wait_recv()

    def forward_operands(blocks):
        for j in range(2):
            v = blocks[j]
            cols = slice(j * v.shape[1], (j + 1) * v.shape[1])
            op_a[:, cols] = v
            op_b[:, cols] = jnp.concatenate([v[16:], -v[:16]], axis=0)

    def adjoint_operands(blocks):
        for j in range(2):
            for k in range(n_mic // 128):
                v = blocks[j, :, k * 128:(k + 1) * 128].astype(F32)
                rows = slice(j * n_mic + k * 128, j * n_mic + (k + 1) * 128)
                col_a[rows, :] = v.T.astype(BF16)
                col_b[rows, :] = jnp.concatenate([-v[16:], v[:16]], axis=0).T.astype(BF16)

    def products(accs, pairs):
        out = []
        for acc, (left, right) in zip(accs, pairs):
            prod = left * right
            out.append(acc + jnp.sum(prod.reshape(4, 8, prod.shape[1]), axis=0))
        return out

    def ex_copy(v, k):
        cols = pl.ds(k * BLOCK, BLOCK)
        return rcopy(part.at[v, :, cols], part_in.at[v, :, cols], ex_ssem.at[v, k], ex_rsem.at[v, k], other_core)

    def adjoint(v):
        for k in range(2 * n_grid // BLOCK):
            rows = slice(k * BLOCK, (k + 1) * BLOCK)
            columns = (jnp.dot(cos_t[rows, :], col_a[...], preferred_element_type=F32)
                       + jnp.dot(sin_t[rows, :], col_b[...], preferred_element_type=F32))
            for m in range(BLOCK // 128):
                low = k * BLOCK + m * 128
                part[v, :, low:low + 128] = columns[m * 128:(m + 1) * 128].T
            ex_copy(v, k).start()
        for k in range(2 * n_grid // BLOCK):
            cols = slice(k * BLOCK, (k + 1) * BLOCK)
            ex_copy(v, k).wait_recv()
            total = part[v, :, cols] + part_in[v, :, cols]
            grad[v, :, cols] = total
            h, low = divmod(k * BLOCK, n_grid)
            grad_half[v, h, :, low:low + BLOCK] = total.astype(BF16)

    def forward(v):
        for k in range(2 * n_mic // BLOCK):
            cols = slice(k * BLOCK, (k + 1) * BLOCK)
            total = (jnp.dot(op_a[...], cos_t[:, cols], preferred_element_type=F32)
                     + jnp.dot(op_b[...], sin_t[:, cols], preferred_element_type=F32))
            image[v, :, cols] = total
            h, low = divmod(k * BLOCK, n_mic)
            image_half[v, h, :, low:low + BLOCK] = total.astype(BF16)

    def sol_copy(v, shift):
        to = z // 2 + shift
        return rcopy(grad_half.at[v, c], sol_in.at[v, z], so_ssem.at[v, shift], so_rsem.at[v, z], dev(c, to, x))

    def own_block(shift):
        return jnp.logical_and(z // 2 + shift == z, c == x)

    def send_sol(v):
        for shift in range(3):
            @pl.when(jnp.logical_not(own_block(shift)))
            def _():
                sol_copy(v, shift).start()

        @pl.when(c == x)
        def _():
            sol_in[v, z] = grad_half[v, c]

    relays = jnp.logical_or(z == 1, z == 2)

    def relay_copy(v, i):
        l = jnp.where(z == 2, i, 2 + i)
        return rcopy(sol_in.at[v, l], sol_in.at[v, l], rl_ssem.at[v, i], so_rsem.at[v, l],
                     dev(x, jnp.where(z == 2, 3, 0), c))

    def relay_sol(v):
        @pl.when(relays)
        def _():
            for i in range(2):
                relay_copy(v, i).wait_recv()
                relay_copy(v, i).start()

    def res_copy(v, j):
        return rcopy(image_half.at[v, j], res_in.at[v, z], re_ssem.at[v, j], re_rsem.at[v, z], dev(x, 2 * c + j, x))

    def own_quarter(j):
        return jnp.logical_and(z == 2 * c + j, c == x)

    def send_res(v):
        for j in range(2):
            @pl.when(jnp.logical_not(own_quarter(j)))
            def _():
                res_copy(v, j).start()

            @pl.when(own_quarter(j))
            def _():
                res_in[v, z] = image_half[v, j]

    def fw_copy(v, l):
        return rcopy(res_in.at[v, l], res_in.at[v, l], fw_ssem.at[v, l], re_rsem.at[v, l], dev(1 - x, z, c))

    def forward_res(v):
        @pl.when(c == x)
        def _():
            for l in range(4):
                @pl.when(jnp.logical_not(jnp.logical_and(z == l, c == half)))
                def _():
                    fw_copy(v, l).wait_recv()
                fw_copy(v, l).start()

    adjoint_operands(p_all)
    adjoint(0)
    send_sol(0)
    forward_operands([grad_half[0, 0], grad_half[0, 1]])
    forward(0)
    send_res(0)
    adjoint_operands(image_half.at[0])
    adjoint(1)
    send_sol(1)
    relay_sol(0)
    forward_operands([grad_half[1, 0], grad_half[1, 1]])
    forward(1)
    send_res(1)
    forward_res(0)
    relay_sol(1)

    zero = jnp.zeros((8, 128), F32)
    accs = [zero] * 6
    for k in range(2 * n_grid // 128):
        cols = slice(k * 128, (k + 1) * 128)
        g, u = grad[0, :, cols], grad[1, :, cols]
        accs[:3] = products(accs[:3], [(g, g), (g, u), (u, u)])
    for k in range(2 * n_mic // 128):
        cols = slice(k * 128, (k + 1) * 128)
        q, w = image[0, :, cols], image[1, :, cols]
        accs[3:] = products(accs[3:], [(q, q), (q, w), (w, w)])
    for i in range(6):
        weight = 0.5 if i < 3 else 1.0
        red_out[i:i + 1, :] = weight * jnp.sum(accs[i], axis=0, keepdims=True)
    red_out[6:8, :] = jnp.zeros((2, 128), F32)

    me = (x * 4 + z) * 2 + c

    def rd_copy(i):
        return rcopy(red_out, red_in.at[me], rd_ssem.at[i], rd_rsem.at[i], at_offset(offsets[i]))

    for i in range(len(offsets)):
        rd_copy(i).start()
    red_in[me] = red_out[...]
    for i in range(len(offsets)):
        rd_copy(i).wait_recv()
    total = red_in[0]
    for i in range(1, len(offsets) + 1):
        total = total + red_in[i]
    red_y[...] = total
    y_copy = rcopy(red_y, red_y_in, ry_sem.at[0], ry_sem.at[1], dev(x, z, c, 1 - y))
    y_copy.start()
    forward_res(1)
    y_copy.wait_recv()
    sums = jnp.sum(red_y[...] + red_y_in[...], axis=1, keepdims=True)
    gg, gu, uu, qq, qw, ww = [sums[i:i + 1, :] for i in range(6)]
    step0 = gg / qq
    next_norm = gg - 2.0 * step0 * gu + step0 * step0 * uu
    grown = 1.0 + next_norm / gg
    image_norm = grown * grown * qq - 2.0 * grown * step0 * qw + step0 * step0 * ww
    step1 = next_norm / image_norm
    first = step0 + step1 * grown
    second = -(step1 * step0)

    for l in range(4):
        for v in range(2):
            relayed = jnp.logical_and(relays, (z == 2) if l < 2 else (z == 1))

            @pl.when(jnp.logical_not(jnp.logical_or(relayed, jnp.logical_and(z == l, c == x))))
            def _():
                rcopy(grad_half.at[v, 0], sol_in.at[v, l], so_ssem.at[v, 0], so_rsem.at[v, l],
                      other_core).wait_recv()
        sol_ref[l] = first * sol_in[0, l].astype(F32) + second * sol_in[1, l].astype(F32)
    for l in range(4):
        @pl.when(c != x)
        def _():
            for v in range(2):
                fw_copy(v, l).wait_recv()
        res_ref[l] = p_loc[l] - (first * res_in[0, l].astype(F32) + second * res_in[1, l].astype(F32))

    gp_copy.wait_send()

    @pl.when(c == half)
    def _():
        for shift in range(1, 4):
            mic_copy(shift).wait_send()

    @pl.when(c == x)
    def _():
        wn_copy.wait_send()
        for shift in range(1, 4):
            p_copy(shift).wait_send()

        @pl.when(c != half)
        def _():
            p_copy(0).wait_send()
        for v in range(2):
            for l in range(4):
                fw_copy(v, l).wait_send()
    for v in range(2):
        for k in range(2 * n_grid // BLOCK):
            ex_copy(v, k).wait_send()
        for shift in range(3):
            @pl.when(jnp.logical_not(own_block(shift)))
            def _():
                sol_copy(v, shift).wait_send()

        @pl.when(relays)
        def _():
            for i in range(2):
                relay_copy(v, i).wait_send()
        for j in range(2):
            @pl.when(jnp.logical_not(own_quarter(j)))
            def _():
                res_copy(v, j).wait_send()
    for i in range(len(offsets)):
        rd_copy(i).wait_send()
    y_copy.wait_send()


def per_chip(grid_points, mic_coords, wavenumbers, pressures):
    bins, parts, snaps, mics = pressures.shape
    rows = parts * snaps
    points = grid_points.shape[1]
    norm_scale = 1.0 / math.sqrt(points * lax.axis_size("grid"))
    vmem = pl.BlockSpec(memory_space=pltpu.VMEM)
    dma = pltpu.SemaphoreType.DMA
    blocks = 2 * points // BLOCK
    solution, residual = pl.pallas_call(
        functools.partial(kernel, norm_scale),
        out_shape=(jax.ShapeDtypeStruct((bins, rows, points), F32), jax.ShapeDtypeStruct((bins, rows, mics), F32)),
        in_specs=[pl.BlockSpec(memory_space=pltpu.HBM)] * 4,
        out_specs=(vmem, vmem),
        scratch_shapes=[
            pltpu.VMEM((2, 3, points), F32),
            pltpu.VMEM((2, 3, mics), F32),
            pltpu.VMEM((1, bins), F32),
            pltpu.VMEM((bins, rows, mics), F32),
            pltpu.VMEM((128, 2 * points), F32),
            pltpu.VMEM((32, 2 * mics), F32),
            pltpu.VMEM((2 * points, 128), BF16),
            pltpu.VMEM((128, 2 * mics), BF16),
            pltpu.VMEM((ROWS, 2 * mics), F32),
            pltpu.VMEM((ROWS, 2 * mics), F32),
            pltpu.VMEM((2 * points, 2 * mics), BF16),
            pltpu.VMEM((2 * points, 2 * mics), BF16),
            pltpu.VMEM((bins, rows, mics), BF16),
            pltpu.VMEM((2, rows, mics), BF16),
            pltpu.VMEM((rows, 2 * mics), BF16),
            pltpu.VMEM((rows, 2 * mics), BF16),
            pltpu.VMEM((2 * mics, rows), BF16),
            pltpu.VMEM((2 * mics, rows), BF16),
            pltpu.VMEM((2, rows, 2 * points), F32),
            pltpu.VMEM((2, rows, 2 * points), F32),
            pltpu.VMEM((2, rows, 2 * points), F32),
            pltpu.VMEM((2, rows, 2 * mics), F32),
            pltpu.VMEM((2, 2, rows, points), BF16),
            pltpu.VMEM((2, 2, rows, mics), BF16),
            pltpu.VMEM((2, bins, rows, points), BF16),
            pltpu.VMEM((2, bins, rows, mics), BF16),
            pltpu.VMEM((8, 128), F32),
            pltpu.VMEM((16, 8, 128), F32),
            pltpu.VMEM((8, 128), F32),
            pltpu.VMEM((8, 128), F32),
            dma((5,)), dma((4,)), dma((4,)), dma((2,)),
            dma((2, blocks)), dma((2, blocks)), dma((2, 4)), dma((2, 4)),
            dma((2, 2)), dma((2, 4)), dma((2, 4)), dma((15,)), dma((15,)), dma((2,)), dma((4,)), dma((2, 2)),
        ],
        compiler_params=pltpu.CompilerParams(
            collective_id=0, has_side_effects=True, vmem_limit_bytes=48 * 1024 * 1024),
    )(grid_points, mic_coords, wavenumbers.reshape(1, bins), pressures.reshape(bins, rows, mics))
    return (solution.reshape(bins, parts, snaps, points), residual.reshape(pressures.shape))


ITERS = 2


def steering_tiles(grid_points, mic_coords, wavenumbers, norm_scale):
    dist_x = grid_points[0][:, None] - mic_coords[0][None, :]
    dist_y = grid_points[1][:, None] - mic_coords[1][None, :]
    dist_z = grid_points[2][:, None] - mic_coords[2][None, :]
    radius = jnp.sqrt(dist_x * dist_x + dist_y * dist_y + dist_z * dist_z)
    amplitude = norm_scale / radius
    cos_list = []
    sin_list = []
    for bin_index in range(wavenumbers.shape[0]):
        phase_angle = wavenumbers[bin_index] * radius
        cos_list.append((jnp.cos(phase_angle) * amplitude).astype(jnp.bfloat16))
        sin_list.append((jnp.sin(phase_angle) * amplitude).astype(jnp.bfloat16))
    return (jnp.stack(cos_list), jnp.stack(sin_list))


def body(grid_points, mic_coords, wavenumbers, pressures):
    bin_count = pressures.shape[0]
    snap_count = pressures.shape[2]
    grid_local = grid_points.shape[1]
    norm_scale = 1.0 / math.sqrt(grid_local * lax.axis_size("grid"))
    cos_tiles, sin_tiles = steering_tiles(grid_points, mic_coords, wavenumbers, norm_scale)

    def combine_adjoint(cos_sum, sin_sum):
        real_part = cos_sum[:, :snap_count] - sin_sum[:, snap_count:]
        imag_part = cos_sum[:, snap_count:] + sin_sum[:, :snap_count]
        return jnp.stack([real_part, imag_part], axis=1)

    def apply_adjoint(residual):
        rounded = residual.astype(jnp.bfloat16).reshape(
            bin_count, 2 * snap_count, residual.shape[3]
        )
        cos_sum = jnp.einsum("fkm,fgm->fkg", rounded, cos_tiles, preferred_element_type=jnp.float32)
        sin_sum = jnp.einsum("fkm,fgm->fkg", rounded, sin_tiles, preferred_element_type=jnp.float32)
        partial_terms = combine_adjoint(cos_sum, sin_sum)
        summed = lax.psum(partial_terms, "mic")
        grad_norm = lax.psum(jnp.sum(summed * summed), ("grid", "bin"))
        return (summed, grad_norm)

    residual = pressures
    gradient, grad_norm = apply_adjoint(residual)
    direction = gradient
    solution = jnp.zeros_like(gradient)
    for iteration in range(ITERS):
        apply_rounded = direction.astype(jnp.bfloat16).reshape(
            bin_count, 2 * snap_count, direction.shape[3]
        )
        apply_cos_sum = jnp.einsum(
            "fkg,fgm->fkm", apply_rounded, cos_tiles, preferred_element_type=jnp.float32
        )
        apply_sin_sum = jnp.einsum(
            "fkg,fgm->fkm", apply_rounded, sin_tiles, preferred_element_type=jnp.float32
        )
        combine_real_part = apply_cos_sum[:, :snap_count] + apply_sin_sum[:, snap_count:]
        combine_imag_part = apply_cos_sum[:, snap_count:] - apply_sin_sum[:, :snap_count]
        apply_partial_terms = jnp.stack([combine_real_part, combine_imag_part], axis=1)
        apply_summed = lax.psum(apply_partial_terms, "grid")
        image_norm = lax.psum(jnp.sum(apply_summed * apply_summed), ("mic", "bin"))
        image, image_norm = (apply_summed, image_norm)
        step_size = grad_norm / image_norm
        solution = solution + step_size * direction
        residual = residual - step_size * image
        if iteration + 1 < ITERS:
            gradient, next_norm = apply_adjoint(residual)
            direction = gradient + next_norm / grad_norm * direction
            grad_norm = next_norm
    return (solution, residual)


def solution(mesh):
    placed = (P(None, "grid"), P(None, "mic"), P("bin"), P("bin", None, None, "mic"))
    sizes = (mesh.shape["grid"], mesh.shape["mic"], mesh.shape["bin"])
    return jax.shard_map(
        per_chip if sizes == (2, 4, 4) else body,
        mesh=mesh,
        in_specs=placed,
        out_specs=(P("bin", None, None, "grid"), P("bin", None, None, "mic")),
        check_vma=False,
    )
```

```python
import functools
import math

import jax
import jax.numpy as jnp
from jax import lax
from jax.experimental import pallas as pl
from jax.experimental.pallas import tpu as pltpu
from jax.sharding import PartitionSpec as P

MESH = pl.DeviceIdType.MESH
F32 = jnp.float32
BF16 = jnp.bfloat16

SIN_COEF = (4.4428679, -7.30744342, 3.59478804, -0.78437393)
COS_COEF = (1.41420408, -6.97764205, 5.71523831, -1.72834838)
ROUNDER = 12582912.0
ROWS = 64
TILE = 256
BLOCK = 512


def poly(coef, s):
    total = coef[-1]
    for value in coef[-2::-1]:
        total = total * s + value
    return total


def kernel(norm_scale, gp_ref, mc_ref, wn_ref, p_ref, sol_ref, res_ref,
           gp_all, mc_all, wn_buf, p_loc, g_rows, m_rows, g_mat, m_mat, cos_t, sin_t, p_send, p_all, op_a, op_b,
           part, part_in, grad, image, grad_half, image_half, sol_in, res_in,
           red_out, red_in, red_y, red_y_in,
           co_send, co_recv, p_ssem, p_rsem, ex_ssem, ex_rsem, so_ssem, so_rsem,
           re_ssem, re_rsem, fw_ssem, rd_ssem, rd_rsem, ry_sem, in_sem, rl_ssem):
    x, z, b = lax.axis_index("grid"), lax.axis_index("mic"), lax.axis_index("bin")
    y, c = b // 2, b % 2
    half = z // 2
    n_mic = mc_ref.shape[1]
    n_grid = gp_ref.shape[1]

    def dev(gx, mz, core, plane=None):
        plane = y if plane is None else plane
        return {"grid": gx, "mic": mz, "bin": plane * 2 + core}

    other_core = dev(x, z, 1 - c)

    def rcopy(src, dst, ssem, rsem, device):
        return pltpu.make_async_remote_copy(
            src_ref=src, dst_ref=dst, send_sem=ssem, recv_sem=rsem, device_id=device, device_id_type=MESH)

    offsets = [(dx, dz, dc) for dx in range(2) for dz in range(4) for dc in range(2)][1:]

    def at_offset(o):
        return dev((x + o[0]) % 2, (z + o[1]) % 4, (c + o[2]) % 2)

    barrier = pltpu.get_barrier_semaphore()
    for o in offsets:
        pl.semaphore_signal(barrier, inc=1, device_id=at_offset(o), device_id_type=MESH)
    pl.semaphore_signal(barrier, inc=1, device_id=dev(x, z, c, 1 - y), device_id_type=MESH)
    p_load = pltpu.make_async_copy(p_ref, p_loc, in_sem.at[0])
    p_load.start()
    gp_load = pltpu.make_async_copy(gp_ref, gp_all.at[x], in_sem.at[1])
    gp_load.start()
    mc_load = pltpu.make_async_copy(mc_ref, mc_all.at[z % 2], in_sem.at[2])
    wn_load = pltpu.make_async_copy(wn_ref, wn_buf, in_sem.at[3])

    @pl.when(c == half)
    def _():
        mc_load.start()

    @pl.when(c == x)
    def _():
        wn_load.start()

    g_rows[...] = jnp.zeros(g_rows.shape, F32)
    m_rows[...] = jnp.zeros(m_rows.shape, F32)
    m_mat[...] = jnp.zeros(m_mat.shape, BF16)
    pl.semaphore_wait(barrier, len(offsets) + 1)

    gp_copy = rcopy(gp_ref, gp_all.at[x], co_send.at[0], co_recv.at[0], dev(1 - x, z, c))
    gp_copy.start()

    def mic_copy(shift):
        return rcopy(mc_ref, mc_all.at[z % 2], co_send.at[1 + shift], co_recv.at[1 + z % 2],
                     dev(x, (z + shift) % 4, c))

    @pl.when(c == half)
    def _():
        for shift in range(1, 4):
            mic_copy(shift).start()

    wn_copy = rcopy(wn_ref, wn_buf, co_send.at[0 + 4], co_recv.at[3], other_core)

    @pl.when(c == x)
    def _():
        wn_copy.start()

    def p_copy(shift):
        to = (z + shift) % 4
        return rcopy(p_send.at[to], p_all.at[z % 2], p_ssem.at[shift], p_rsem.at[z % 2], dev(x, to, half))

    p_load.wait()

    @pl.when(c == x)
    def _():
        p_send[...] = p_loc[...].astype(BF16)
        for shift in range(4):
            if shift:
                p_copy(shift).start()
            else:
                @pl.when(c != half)
                def _():
                    p_copy(0).start()

                @pl.when(c == half)
                def _():
                    p_all[z % 2] = p_send[z]

    gp_load.wait()

    @pl.when(c == half)
    def _():
        mc_load.wait()

    @pl.when(c == x)
    def _():
        wn_load.wait()

    gp_copy.wait_recv()
    for j in range(2):
        @pl.when(z != 2 * c + j)
        def _():
            rcopy(mc_ref, mc_all.at[j], co_send.at[1], co_recv.at[1 + j], other_core).wait_recv()

    @pl.when(c != x)
    def _():
        wn_copy.wait_recv()

    here = lax.broadcasted_iota(jnp.int32, wn_buf.shape, 1) == z
    wavenumber = jnp.sum(jnp.where(here, wn_buf[...], 0.0), axis=1, keepdims=True)
    turns = wavenumber * (1.0 / (2.0 * math.pi))
    scale_row = jnp.broadcast_to(turns * norm_scale, (32, 128))

    def pieces(v):
        high = v.astype(BF16).astype(F32)
        rest = v - high
        mid = rest.astype(BF16).astype(F32)
        return high, mid, (rest - mid).astype(BF16).astype(F32)

    def fill(out, h, width, left, norm_at, one_at, v):
        cols = slice(h * width, (h + 1) * width)
        split = pieces(v)
        for i, which in enumerate(left):
            out[3 * i:3 * i + 3, cols] = split[which]
        for i, value in enumerate(pieces(jnp.sum(v * v, axis=0, keepdims=True))):
            out[norm_at + i:norm_at + i + 1, cols] = value
        out[one_at:one_at + 3, cols] = jnp.ones((3, width), F32)

    for h in range(2):
        fill(g_rows, h, n_grid, (0, 0, 1, 1, 0, 2), 18, 21, gp_all[h] * turns)
        fill(m_rows, h, n_mic, (0, 1, 0, 1, 2, 0), 21, 18, mc_all[h] * turns)
    row_index = lax.broadcasted_iota(jnp.int32, (32, 1), 0)
    m_mat[0:32, :] = (m_rows[...] * jnp.where(row_index < 18, -2.0, 1.0)).astype(BF16)
    for k in range(2 * n_grid // 128):
        g_mat[k * 128:(k + 1) * 128, :] = g_rows[:, k * 128:(k + 1) * 128].T.astype(BF16)

    @pl.loop(0, 2 * n_grid // ROWS)
    def _(i):
        base = pl.multiple_of(i * ROWS, ROWS)
        points = g_mat[pl.ds(base, ROWS), :]
        for n in range(2 * n_mic // TILE):
            squares = jnp.dot(points, m_mat[:, n * TILE:(n + 1) * TILE], preferred_element_type=F32)
            for r in range(ROWS // 32):
                for k in range(TILE // 128):
                    q = squares[r * 32:(r + 1) * 32, k * 128:(k + 1) * 128]
                    inv = lax.rsqrt(q)
                    t = q * inv
                    amp = inv * scale_row
                    f = t - ((t + ROUNDER) - ROUNDER)
                    s = f * f
                    sine = f * poly(SIN_COEF, s)
                    cosine = poly(COS_COEF, s)
                    scaled = sine * amp
                    rows = pl.ds(base + r * 32, 32)
                    cols = slice(n * TILE + k * 128, n * TILE + (k + 1) * 128)
                    cos_t[rows, cols] = (amp - scaled * sine).astype(BF16)
                    sin_t[rows, cols] = (scaled * cosine).astype(BF16)

    for j in range(2):
        @pl.when(jnp.logical_not(jnp.logical_and(z == 2 * c + j, c == x)))
        def _():
            rcopy(p_send.at[0], p_all.at[j], p_ssem.at[0], p_rsem.at[j], other_core).wait_recv()

    def operands(blocks, adjoint):
        for j in range(2):
            v = blocks[j]
            real, imag = v[:16], v[16:]
            swapped = [-imag, real] if adjoint else [imag, -real]
            cols = slice(j * v.shape[1], (j + 1) * v.shape[1])
            op_a[:, cols] = v
            op_b[:, cols] = jnp.concatenate(swapped, axis=0)

    def products(accs, pairs):
        out = []
        for acc, (left, right) in zip(accs, pairs):
            prod = left * right
            out.append(acc + jnp.sum(prod.reshape(4, 8, prod.shape[1]), axis=0))
        return out

    def ex_copy(v, k):
        cols = pl.ds(k * BLOCK, BLOCK)
        return rcopy(part.at[v, :, cols], part_in.at[v, :, cols], ex_ssem.at[v, k], ex_rsem.at[v, k], other_core)

    def adjoint(v):
        for k in range(2 * n_grid // BLOCK):
            rows = slice(k * BLOCK, (k + 1) * BLOCK)
            dims = (((1,), (1,)), ((), ()))
            part[v, :, rows] = (
                lax.dot_general(op_a[...], cos_t[rows, :], dims, preferred_element_type=F32)
                + lax.dot_general(op_b[...], sin_t[rows, :], dims, preferred_element_type=F32))
            ex_copy(v, k).start()
        for k in range(2 * n_grid // BLOCK):
            cols = slice(k * BLOCK, (k + 1) * BLOCK)
            ex_copy(v, k).wait_recv()
            total = part[v, :, cols] + part_in[v, :, cols]
            grad[v, :, cols] = total
            h, low = divmod(k * BLOCK, n_grid)
            grad_half[v, h, :, low:low + BLOCK] = total.astype(BF16)

    def forward(v):
        for k in range(2 * n_mic // BLOCK):
            cols = slice(k * BLOCK, (k + 1) * BLOCK)
            total = (jnp.dot(op_a[...], cos_t[:, cols], preferred_element_type=F32)
                     + jnp.dot(op_b[...], sin_t[:, cols], preferred_element_type=F32))
            image[v, :, cols] = total
            h, low = divmod(k * BLOCK, n_mic)
            image_half[v, h, :, low:low + BLOCK] = total.astype(BF16)

    def sol_copy(v, shift):
        to = z // 2 + shift
        return rcopy(grad_half.at[v, c], sol_in.at[v, z], so_ssem.at[v, shift], so_rsem.at[v, z], dev(c, to, x))

    def own_block(shift):
        return jnp.logical_and(z // 2 + shift == z, c == x)

    def send_sol(v):
        for shift in range(3):
            @pl.when(jnp.logical_not(own_block(shift)))
            def _():
                sol_copy(v, shift).start()

        @pl.when(c == x)
        def _():
            sol_in[v, z] = grad_half[v, c]

    relays = jnp.logical_or(z == 1, z == 2)

    def relay_copy(v, i):
        l = jnp.where(z == 2, i, 2 + i)
        return rcopy(sol_in.at[v, l], sol_in.at[v, l], rl_ssem.at[v, i], so_rsem.at[v, l],
                     dev(x, jnp.where(z == 2, 3, 0), c))

    def relay_sol(v):
        @pl.when(relays)
        def _():
            for i in range(2):
                relay_copy(v, i).wait_recv()
                relay_copy(v, i).start()

    def res_copy(v, j):
        return rcopy(image_half.at[v, j], res_in.at[v, z], re_ssem.at[v, j], re_rsem.at[v, z], dev(x, 2 * c + j, x))

    def own_quarter(j):
        return jnp.logical_and(z == 2 * c + j, c == x)

    def send_res(v):
        for j in range(2):
            @pl.when(jnp.logical_not(own_quarter(j)))
            def _():
                res_copy(v, j).start()

            @pl.when(own_quarter(j))
            def _():
                res_in[v, z] = image_half[v, j]

    def fw_copy(v, l):
        return rcopy(res_in.at[v, l], res_in.at[v, l], fw_ssem.at[v, l], re_rsem.at[v, l], dev(1 - x, z, c))

    def forward_res(v):
        @pl.when(c == x)
        def _():
            for l in range(4):
                @pl.when(jnp.logical_not(jnp.logical_and(z == l, c == half)))
                def _():
                    fw_copy(v, l).wait_recv()
                fw_copy(v, l).start()

    operands([p_all[0], p_all[1]], True)
    adjoint(0)
    send_sol(0)
    operands([grad_half[0, 0], grad_half[0, 1]], False)
    forward(0)
    send_res(0)
    operands([image_half[0, 0], image_half[0, 1]], True)
    adjoint(1)
    send_sol(1)
    relay_sol(0)
    operands([grad_half[1, 0], grad_half[1, 1]], False)
    forward(1)

    zero = jnp.zeros((8, 128), F32)
    accs = [zero] * 6
    for k in range(2 * n_grid // 128):
        cols = slice(k * 128, (k + 1) * 128)
        g, u = grad[0, :, cols], grad[1, :, cols]
        accs[:3] = products(accs[:3], [(g, g), (g, u), (u, u)])
    for k in range(2 * n_mic // 128):
        cols = slice(k * 128, (k + 1) * 128)
        q, w = image[0, :, cols], image[1, :, cols]
        accs[3:] = products(accs[3:], [(q, q), (q, w), (w, w)])
    for i in range(6):
        weight = 0.5 if i < 3 else 1.0
        red_out[i:i + 1, :] = weight * jnp.sum(accs[i], axis=0, keepdims=True)
    red_out[6:8, :] = jnp.zeros((2, 128), F32)

    me = (x * 4 + z) * 2 + c

    def rd_copy(i):
        return rcopy(red_out, red_in.at[me], rd_ssem.at[i], rd_rsem.at[i], at_offset(offsets[i]))

    for i in range(len(offsets)):
        rd_copy(i).start()
    send_res(1)
    forward_res(0)
    relay_sol(1)
    red_in[me] = red_out[...]
    for i in range(len(offsets)):
        rd_copy(i).wait_recv()
    total = red_in[0]
    for i in range(1, len(offsets) + 1):
        total = total + red_in[i]
    red_y[...] = total
    y_copy = rcopy(red_y, red_y_in, ry_sem.at[0], ry_sem.at[1], dev(x, z, c, 1 - y))
    y_copy.start()
    forward_res(1)
    y_copy.wait_recv()
    sums = jnp.sum(red_y[...] + red_y_in[...], axis=1, keepdims=True)
    gg, gu, uu, qq, qw, ww = [sums[i:i + 1, :] for i in range(6)]
    step0 = gg / qq
    next_norm = gg - 2.0 * step0 * gu + step0 * step0 * uu
    grown = 1.0 + next_norm / gg
    image_norm = grown * grown * qq - 2.0 * grown * step0 * qw + step0 * step0 * ww
    step1 = next_norm / image_norm
    first = step0 + step1 * grown
    second = -(step1 * step0)

    for l in range(4):
        for v in range(2):
            relayed = jnp.logical_and(relays, (z == 2) if l < 2 else (z == 1))

            @pl.when(jnp.logical_not(jnp.logical_or(relayed, jnp.logical_and(z == l, c == x))))
            def _():
                rcopy(grad_half.at[v, 0], sol_in.at[v, l], so_ssem.at[v, 0], so_rsem.at[v, l],
                      other_core).wait_recv()
        sol_ref[l] = first * sol_in[0, l].astype(F32) + second * sol_in[1, l].astype(F32)
    for l in range(4):
        @pl.when(c != x)
        def _():
            for v in range(2):
                fw_copy(v, l).wait_recv()
        res_ref[l] = p_loc[l] - (first * res_in[0, l].astype(F32) + second * res_in[1, l].astype(F32))

    gp_copy.wait_send()

    @pl.when(c == half)
    def _():
        for shift in range(1, 4):
            mic_copy(shift).wait_send()

    @pl.when(c == x)
    def _():
        wn_copy.wait_send()
        for shift in range(1, 4):
            p_copy(shift).wait_send()

        @pl.when(c != half)
        def _():
            p_copy(0).wait_send()
        for v in range(2):
            for l in range(4):
                fw_copy(v, l).wait_send()
    for v in range(2):
        for k in range(2 * n_grid // BLOCK):
            ex_copy(v, k).wait_send()
        for shift in range(3):
            @pl.when(jnp.logical_not(own_block(shift)))
            def _():
                sol_copy(v, shift).wait_send()

        @pl.when(relays)
        def _():
            for i in range(2):
                relay_copy(v, i).wait_send()
        for j in range(2):
            @pl.when(jnp.logical_not(own_quarter(j)))
            def _():
                res_copy(v, j).wait_send()
    for i in range(len(offsets)):
        rd_copy(i).wait_send()
    y_copy.wait_send()


def per_chip(grid_points, mic_coords, wavenumbers, pressures):
    bins, parts, snaps, mics = pressures.shape
    rows = parts * snaps
    points = grid_points.shape[1]
    norm_scale = 1.0 / math.sqrt(points * lax.axis_size("grid"))
    vmem = pl.BlockSpec(memory_space=pltpu.VMEM)
    dma = pltpu.SemaphoreType.DMA
    blocks = 2 * points // BLOCK
    solution, residual = pl.pallas_call(
        functools.partial(kernel, norm_scale),
        out_shape=(jax.ShapeDtypeStruct((bins, rows, points), F32), jax.ShapeDtypeStruct((bins, rows, mics), F32)),
        in_specs=[pl.BlockSpec(memory_space=pltpu.HBM)] * 4,
        out_specs=(vmem, vmem),
        scratch_shapes=[
            pltpu.VMEM((2, 3, points), F32),
            pltpu.VMEM((2, 3, mics), F32),
            pltpu.VMEM((1, bins), F32),
            pltpu.VMEM((bins, rows, mics), F32),
            pltpu.VMEM((128, 2 * points), F32),
            pltpu.VMEM((32, 2 * mics), F32),
            pltpu.VMEM((2 * points, 128), BF16),
            pltpu.VMEM((128, 2 * mics), BF16),
            pltpu.VMEM((2 * points, 2 * mics), BF16),
            pltpu.VMEM((2 * points, 2 * mics), BF16),
            pltpu.VMEM((bins, rows, mics), BF16),
            pltpu.VMEM((2, rows, mics), BF16),
            pltpu.VMEM((rows, 2 * mics), BF16),
            pltpu.VMEM((rows, 2 * mics), BF16),
            pltpu.VMEM((2, rows, 2 * points), F32),
            pltpu.VMEM((2, rows, 2 * points), F32),
            pltpu.VMEM((2, rows, 2 * points), F32),
            pltpu.VMEM((2, rows, 2 * mics), F32),
            pltpu.VMEM((2, 2, rows, points), BF16),
            pltpu.VMEM((2, 2, rows, mics), BF16),
            pltpu.VMEM((2, bins, rows, points), BF16),
            pltpu.VMEM((2, bins, rows, mics), BF16),
            pltpu.VMEM((8, 128), F32),
            pltpu.VMEM((16, 8, 128), F32),
            pltpu.VMEM((8, 128), F32),
            pltpu.VMEM((8, 128), F32),
            dma((5,)), dma((4,)), dma((4,)), dma((2,)),
            dma((2, blocks)), dma((2, blocks)), dma((2, 4)), dma((2, 4)),
            dma((2, 2)), dma((2, 4)), dma((2, 4)), dma((15,)), dma((15,)), dma((2,)), dma((4,)), dma((2, 2)),
        ],
        compiler_params=pltpu.CompilerParams(
            collective_id=0, has_side_effects=True, vmem_limit_bytes=48 * 1024 * 1024),
    )(grid_points, mic_coords, wavenumbers.reshape(1, bins), pressures.reshape(bins, rows, mics))
    return (solution.reshape(bins, parts, snaps, points), residual.reshape(pressures.shape))


ITERS = 2


def steering_tiles(grid_points, mic_coords, wavenumbers, norm_scale):
    dist_x = grid_points[0][:, None] - mic_coords[0][None, :]
    dist_y = grid_points[1][:, None] - mic_coords[1][None, :]
    dist_z = grid_points[2][:, None] - mic_coords[2][None, :]
    radius = jnp.sqrt(dist_x * dist_x + dist_y * dist_y + dist_z * dist_z)
    amplitude = norm_scale / radius
    cos_list = []
    sin_list = []
    for bin_index in range(wavenumbers.shape[0]):
        phase_angle = wavenumbers[bin_index] * radius
        cos_list.append((jnp.cos(phase_angle) * amplitude).astype(jnp.bfloat16))
        sin_list.append((jnp.sin(phase_angle) * amplitude).astype(jnp.bfloat16))
    return (jnp.stack(cos_list), jnp.stack(sin_list))


def body(grid_points, mic_coords, wavenumbers, pressures):
    bin_count = pressures.shape[0]
    snap_count = pressures.shape[2]
    grid_local = grid_points.shape[1]
    norm_scale = 1.0 / math.sqrt(grid_local * lax.axis_size("grid"))
    cos_tiles, sin_tiles = steering_tiles(grid_points, mic_coords, wavenumbers, norm_scale)

    def combine_adjoint(cos_sum, sin_sum):
        real_part = cos_sum[:, :snap_count] - sin_sum[:, snap_count:]
        imag_part = cos_sum[:, snap_count:] + sin_sum[:, :snap_count]
        return jnp.stack([real_part, imag_part], axis=1)

    def apply_adjoint(residual):
        rounded = residual.astype(jnp.bfloat16).reshape(
            bin_count, 2 * snap_count, residual.shape[3]
        )
        cos_sum = jnp.einsum("fkm,fgm->fkg", rounded, cos_tiles, preferred_element_type=jnp.float32)
        sin_sum = jnp.einsum("fkm,fgm->fkg", rounded, sin_tiles, preferred_element_type=jnp.float32)
        partial_terms = combine_adjoint(cos_sum, sin_sum)
        summed = lax.psum(partial_terms, "mic")
        grad_norm = lax.psum(jnp.sum(summed * summed), ("grid", "bin"))
        return (summed, grad_norm)

    residual = pressures
    gradient, grad_norm = apply_adjoint(residual)
    direction = gradient
    solution = jnp.zeros_like(gradient)
    for iteration in range(ITERS):
        apply_rounded = direction.astype(jnp.bfloat16).reshape(
            bin_count, 2 * snap_count, direction.shape[3]
        )
        apply_cos_sum = jnp.einsum(
            "fkg,fgm->fkm", apply_rounded, cos_tiles, preferred_element_type=jnp.float32
        )
        apply_sin_sum = jnp.einsum(
            "fkg,fgm->fkm", apply_rounded, sin_tiles, preferred_element_type=jnp.float32
        )
        combine_real_part = apply_cos_sum[:, :snap_count] + apply_sin_sum[:, snap_count:]
        combine_imag_part = apply_cos_sum[:, snap_count:] - apply_sin_sum[:, :snap_count]
        apply_partial_terms = jnp.stack([combine_real_part, combine_imag_part], axis=1)
        apply_summed = lax.psum(apply_partial_terms, "grid")
        image_norm = lax.psum(jnp.sum(apply_summed * apply_summed), ("mic", "bin"))
        image, image_norm = (apply_summed, image_norm)
        step_size = grad_norm / image_norm
        solution = solution + step_size * direction
        residual = residual - step_size * image
        if iteration + 1 < ITERS:
            gradient, next_norm = apply_adjoint(residual)
            direction = gradient + next_norm / grad_norm * direction
            grad_norm = next_norm
    return (solution, residual)


def solution(mesh):
    placed = (P(None, "grid"), P(None, "mic"), P("bin"), P("bin", None, None, "mic"))
    sizes = (mesh.shape["grid"], mesh.shape["mic"], mesh.shape["bin"])
    return jax.shard_map(
        per_chip if sizes == (2, 4, 4) else body,
        mesh=mesh,
        in_specs=placed,
        out_specs=(P("bin", None, None, "grid"), P("bin", None, None, "mic")),
        check_vma=False,
    )
```

```python
import functools
import math

import jax
import jax.numpy as jnp
from jax import lax
from jax.experimental import pallas as pl
from jax.experimental.pallas import tpu as pltpu
from jax.sharding import PartitionSpec as P

MESH = pl.DeviceIdType.MESH
F32 = jnp.float32
BF16 = jnp.bfloat16

SIN_COEF = (4.4428679, -7.30744342, 3.59478804, -0.78437393)
COS_COEF = (1.41420408, -6.97764205, 5.71523831, -1.72834838)
ROUNDER = 12582912.0
ROWS = 128
TILE = 256
BLOCK = 512


def poly(coef, s):
    total = coef[-1]
    for value in coef[-2::-1]:
        total = total * s + value
    return total


def kernel(norm_scale, gp_ref, mc_ref, wn_ref, p_ref, sol_ref, res_ref,
           gp_all, mc_all, wn_buf, p_loc, g_rows, m_rows, g_mat, m_mat, cos_t, sin_t, p_send, p_all, op_a, op_b,
           part, part_in, grad, image, grad_half, image_half, sol_in, res_in,
           red_out, red_in, red_y, red_y_in,
           co_send, co_recv, p_ssem, p_rsem, ex_ssem, ex_rsem, so_ssem, so_rsem,
           re_ssem, re_rsem, fw_ssem, rd_ssem, rd_rsem, ry_sem, in_sem, rl_ssem):
    x, z, b = lax.axis_index("grid"), lax.axis_index("mic"), lax.axis_index("bin")
    y, c = b // 2, b % 2
    half = z // 2
    n_mic = mc_ref.shape[1]
    n_grid = gp_ref.shape[1]

    def dev(gx, mz, core, plane=None):
        plane = y if plane is None else plane
        return {"grid": gx, "mic": mz, "bin": plane * 2 + core}

    other_core = dev(x, z, 1 - c)

    def rcopy(src, dst, ssem, rsem, device):
        return pltpu.make_async_remote_copy(
            src_ref=src, dst_ref=dst, send_sem=ssem, recv_sem=rsem, device_id=device, device_id_type=MESH)

    offsets = [(dx, dz, dc) for dx in range(2) for dz in range(4) for dc in range(2)][1:]

    def at_offset(o):
        return dev((x + o[0]) % 2, (z + o[1]) % 4, (c + o[2]) % 2)

    barrier = pltpu.get_barrier_semaphore()
    for o in offsets:
        pl.semaphore_signal(barrier, inc=1, device_id=at_offset(o), device_id_type=MESH)
    pl.semaphore_signal(barrier, inc=1, device_id=dev(x, z, c, 1 - y), device_id_type=MESH)
    p_load = pltpu.make_async_copy(p_ref, p_loc, in_sem.at[0])
    p_load.start()
    gp_load = pltpu.make_async_copy(gp_ref, gp_all.at[x], in_sem.at[1])
    gp_load.start()
    mc_load = pltpu.make_async_copy(mc_ref, mc_all.at[z % 2], in_sem.at[2])
    wn_load = pltpu.make_async_copy(wn_ref, wn_buf, in_sem.at[3])

    @pl.when(c == half)
    def _():
        mc_load.start()

    @pl.when(c == x)
    def _():
        wn_load.start()

    g_rows[...] = jnp.zeros(g_rows.shape, F32)
    m_rows[...] = jnp.zeros(m_rows.shape, F32)
    m_mat[...] = jnp.zeros(m_mat.shape, BF16)
    pl.semaphore_wait(barrier, len(offsets) + 1)

    gp_copy = rcopy(gp_ref, gp_all.at[x], co_send.at[0], co_recv.at[0], dev(1 - x, z, c))
    gp_copy.start()

    def mic_copy(shift):
        return rcopy(mc_ref, mc_all.at[z % 2], co_send.at[1 + shift], co_recv.at[1 + z % 2],
                     dev(x, (z + shift) % 4, c))

    @pl.when(c == half)
    def _():
        for shift in range(1, 4):
            mic_copy(shift).start()

    wn_copy = rcopy(wn_ref, wn_buf, co_send.at[0 + 4], co_recv.at[3], other_core)

    @pl.when(c == x)
    def _():
        wn_copy.start()

    def p_copy(shift):
        to = (z + shift) % 4
        return rcopy(p_send.at[to], p_all.at[z % 2], p_ssem.at[shift], p_rsem.at[z % 2], dev(x, to, half))

    p_load.wait()

    @pl.when(c == x)
    def _():
        p_send[...] = p_loc[...].astype(BF16)
        for shift in range(4):
            if shift:
                p_copy(shift).start()
            else:
                @pl.when(c != half)
                def _():
                    p_copy(0).start()

                @pl.when(c == half)
                def _():
                    p_all[z % 2] = p_send[z]

    gp_load.wait()

    @pl.when(c == half)
    def _():
        mc_load.wait()

    @pl.when(c == x)
    def _():
        wn_load.wait()

    gp_copy.wait_recv()
    for j in range(2):
        @pl.when(z != 2 * c + j)
        def _():
            rcopy(mc_ref, mc_all.at[j], co_send.at[1], co_recv.at[1 + j], other_core).wait_recv()

    @pl.when(c != x)
    def _():
        wn_copy.wait_recv()

    here = lax.broadcasted_iota(jnp.int32, wn_buf.shape, 1) == z
    wavenumber = jnp.sum(jnp.where(here, wn_buf[...], 0.0), axis=1, keepdims=True)
    turns = wavenumber * (1.0 / (2.0 * math.pi))
    scale_row = jnp.broadcast_to(turns * norm_scale, (32, 128))

    def pieces(v):
        high = v.astype(BF16).astype(F32)
        rest = v - high
        mid = rest.astype(BF16).astype(F32)
        return high, mid, (rest - mid).astype(BF16).astype(F32)

    def fill(out, h, width, left, norm_at, one_at, v):
        cols = slice(h * width, (h + 1) * width)
        split = pieces(v)
        for i, which in enumerate(left):
            out[3 * i:3 * i + 3, cols] = split[which]
        for i, value in enumerate(pieces(jnp.sum(v * v, axis=0, keepdims=True))):
            out[norm_at + i:norm_at + i + 1, cols] = value
        out[one_at:one_at + 3, cols] = jnp.ones((3, width), F32)

    for h in range(2):
        fill(g_rows, h, n_grid, (0, 0, 1, 1, 0, 2), 18, 21, gp_all[h] * turns)
        fill(m_rows, h, n_mic, (0, 1, 0, 1, 2, 0), 21, 18, mc_all[h] * turns)
    row_index = lax.broadcasted_iota(jnp.int32, (32, 1), 0)
    m_mat[0:32, :] = (m_rows[...] * jnp.where(row_index < 18, -2.0, 1.0)).astype(BF16)
    for k in range(2 * n_grid // 128):
        g_mat[k * 128:(k + 1) * 128, :] = g_rows[:, k * 128:(k + 1) * 128].T.astype(BF16)

    @pl.loop(0, 2 * n_grid // ROWS)
    def _(i):
        base = pl.multiple_of(i * ROWS, ROWS)
        points = g_mat[pl.ds(base, ROWS), :]
        for n in range(2 * n_mic // TILE):
            squares = jnp.dot(points, m_mat[:, n * TILE:(n + 1) * TILE], preferred_element_type=F32)
            for r in range(ROWS // 32):
                for k in range(TILE // 128):
                    q = squares[r * 32:(r + 1) * 32, k * 128:(k + 1) * 128]
                    inv = lax.rsqrt(q)
                    t = q * inv
                    amp = inv * scale_row
                    f = t - ((t + ROUNDER) - ROUNDER)
                    s = f * f
                    sine = f * poly(SIN_COEF, s)
                    cosine = poly(COS_COEF, s)
                    scaled = sine * amp
                    rows = pl.ds(base + r * 32, 32)
                    cols = slice(n * TILE + k * 128, n * TILE + (k + 1) * 128)
                    cos_t[rows, cols] = (amp - scaled * sine).astype(BF16)
                    sin_t[rows, cols] = (scaled * cosine).astype(BF16)

    for j in range(2):
        @pl.when(jnp.logical_not(jnp.logical_and(z == 2 * c + j, c == x)))
        def _():
            rcopy(p_send.at[0], p_all.at[j], p_ssem.at[0], p_rsem.at[j], other_core).wait_recv()

    def operands(blocks, adjoint):
        for j in range(2):
            v = blocks[j]
            real, imag = v[:16], v[16:]
            swapped = [-imag, real] if adjoint else [imag, -real]
            cols = slice(j * v.shape[1], (j + 1) * v.shape[1])
            op_a[:, cols] = v
            op_b[:, cols] = jnp.concatenate(swapped, axis=0)

    def products(accs, pairs):
        out = []
        for acc, (left, right) in zip(accs, pairs):
            prod = left * right
            out.append(acc + jnp.sum(prod.reshape(4, 8, prod.shape[1]), axis=0))
        return out

    def ex_copy(v, k):
        cols = pl.ds(k * BLOCK, BLOCK)
        return rcopy(part.at[v, :, cols], part_in.at[v, :, cols], ex_ssem.at[v, k], ex_rsem.at[v, k], other_core)

    def adjoint(v):
        for k in range(2 * n_grid // BLOCK):
            rows = slice(k * BLOCK, (k + 1) * BLOCK)
            dims = (((1,), (1,)), ((), ()))
            part[v, :, rows] = (
                lax.dot_general(op_a[...], cos_t[rows, :], dims, preferred_element_type=F32)
                + lax.dot_general(op_b[...], sin_t[rows, :], dims, preferred_element_type=F32))
            ex_copy(v, k).start()
        for k in range(2 * n_grid // BLOCK):
            cols = slice(k * BLOCK, (k + 1) * BLOCK)
            ex_copy(v, k).wait_recv()
            total = part[v, :, cols] + part_in[v, :, cols]
            grad[v, :, cols] = total
            h, low = divmod(k * BLOCK, n_grid)
            grad_half[v, h, :, low:low + BLOCK] = total.astype(BF16)

    def forward(v):
        for k in range(2 * n_mic // BLOCK):
            cols = slice(k * BLOCK, (k + 1) * BLOCK)
            total = (jnp.dot(op_a[...], cos_t[:, cols], preferred_element_type=F32)
                     + jnp.dot(op_b[...], sin_t[:, cols], preferred_element_type=F32))
            image[v, :, cols] = total
            h, low = divmod(k * BLOCK, n_mic)
            image_half[v, h, :, low:low + BLOCK] = total.astype(BF16)

    def sol_copy(v, shift):
        to = z // 2 + shift
        return rcopy(grad_half.at[v, c], sol_in.at[v, z], so_ssem.at[v, shift], so_rsem.at[v, z], dev(c, to, x))

    def own_block(shift):
        return jnp.logical_and(z // 2 + shift == z, c == x)

    def send_sol(v):
        for shift in range(3):
            @pl.when(jnp.logical_not(own_block(shift)))
            def _():
                sol_copy(v, shift).start()

        @pl.when(c == x)
        def _():
            sol_in[v, z] = grad_half[v, c]

    relays = jnp.logical_or(z == 1, z == 2)

    def relay_copy(v, i):
        l = jnp.where(z == 2, i, 2 + i)
        return rcopy(sol_in.at[v, l], sol_in.at[v, l], rl_ssem.at[v, i], so_rsem.at[v, l],
                     dev(x, jnp.where(z == 2, 3, 0), c))

    def relay_sol(v):
        @pl.when(relays)
        def _():
            for i in range(2):
                relay_copy(v, i).wait_recv()
                relay_copy(v, i).start()

    def res_copy(v, j):
        return rcopy(image_half.at[v, j], res_in.at[v, z], re_ssem.at[v, j], re_rsem.at[v, z], dev(x, 2 * c + j, x))

    def own_quarter(j):
        return jnp.logical_and(z == 2 * c + j, c == x)

    def send_res(v):
        for j in range(2):
            @pl.when(jnp.logical_not(own_quarter(j)))
            def _():
                res_copy(v, j).start()

            @pl.when(own_quarter(j))
            def _():
                res_in[v, z] = image_half[v, j]

    def fw_copy(v, l):
        return rcopy(res_in.at[v, l], res_in.at[v, l], fw_ssem.at[v, l], re_rsem.at[v, l], dev(1 - x, z, c))

    def forward_res(v):
        @pl.when(c == x)
        def _():
            for l in range(4):
                @pl.when(jnp.logical_not(jnp.logical_and(z == l, c == half)))
                def _():
                    fw_copy(v, l).wait_recv()
                fw_copy(v, l).start()

    operands([p_all[0], p_all[1]], True)
    adjoint(0)
    send_sol(0)
    operands([grad_half[0, 0], grad_half[0, 1]], False)
    forward(0)
    send_res(0)
    operands([image_half[0, 0], image_half[0, 1]], True)
    adjoint(1)
    send_sol(1)
    relay_sol(0)
    operands([grad_half[1, 0], grad_half[1, 1]], False)
    forward(1)

    zero = jnp.zeros((8, 128), F32)
    accs = [zero] * 6
    for k in range(2 * n_grid // 128):
        cols = slice(k * 128, (k + 1) * 128)
        g, u = grad[0, :, cols], grad[1, :, cols]
        accs[:3] = products(accs[:3], [(g, g), (g, u), (u, u)])
    for k in range(2 * n_mic // 128):
        cols = slice(k * 128, (k + 1) * 128)
        q, w = image[0, :, cols], image[1, :, cols]
        accs[3:] = products(accs[3:], [(q, q), (q, w), (w, w)])
    for i in range(6):
        weight = 0.5 if i < 3 else 1.0
        red_out[i:i + 1, :] = weight * jnp.sum(accs[i], axis=0, keepdims=True)
    red_out[6:8, :] = jnp.zeros((2, 128), F32)

    me = (x * 4 + z) * 2 + c

    def rd_copy(i):
        return rcopy(red_out, red_in.at[me], rd_ssem.at[i], rd_rsem.at[i], at_offset(offsets[i]))

    for i in range(len(offsets)):
        rd_copy(i).start()
    send_res(1)
    forward_res(0)
    relay_sol(1)
    red_in[me] = red_out[...]
    for i in range(len(offsets)):
        rd_copy(i).wait_recv()
    total = red_in[0]
    for i in range(1, len(offsets) + 1):
        total = total + red_in[i]
    red_y[...] = total
    y_copy = rcopy(red_y, red_y_in, ry_sem.at[0], ry_sem.at[1], dev(x, z, c, 1 - y))
    y_copy.start()
    forward_res(1)
    y_copy.wait_recv()
    sums = jnp.sum(red_y[...] + red_y_in[...], axis=1, keepdims=True)
    gg, gu, uu, qq, qw, ww = [sums[i:i + 1, :] for i in range(6)]
    step0 = gg / qq
    next_norm = gg - 2.0 * step0 * gu + step0 * step0 * uu
    grown = 1.0 + next_norm / gg
    image_norm = grown * grown * qq - 2.0 * grown * step0 * qw + step0 * step0 * ww
    step1 = next_norm / image_norm
    first = step0 + step1 * grown
    second = -(step1 * step0)

    for l in range(4):
        for v in range(2):
            relayed = jnp.logical_and(relays, (z == 2) if l < 2 else (z == 1))

            @pl.when(jnp.logical_not(jnp.logical_or(relayed, jnp.logical_and(z == l, c == x))))
            def _():
                rcopy(grad_half.at[v, 0], sol_in.at[v, l], so_ssem.at[v, 0], so_rsem.at[v, l],
                      other_core).wait_recv()
        sol_ref[l] = first * sol_in[0, l].astype(F32) + second * sol_in[1, l].astype(F32)
    for l in range(4):
        @pl.when(c != x)
        def _():
            for v in range(2):
                fw_copy(v, l).wait_recv()
        res_ref[l] = p_loc[l] - (first * res_in[0, l].astype(F32) + second * res_in[1, l].astype(F32))

    gp_copy.wait_send()

    @pl.when(c == half)
    def _():
        for shift in range(1, 4):
            mic_copy(shift).wait_send()

    @pl.when(c == x)
    def _():
        wn_copy.wait_send()
        for shift in range(1, 4):
            p_copy(shift).wait_send()

        @pl.when(c != half)
        def _():
            p_copy(0).wait_send()
        for v in range(2):
            for l in range(4):
                fw_copy(v, l).wait_send()
    for v in range(2):
        for k in range(2 * n_grid // BLOCK):
            ex_copy(v, k).wait_send()
        for shift in range(3):
            @pl.when(jnp.logical_not(own_block(shift)))
            def _():
                sol_copy(v, shift).wait_send()

        @pl.when(relays)
        def _():
            for i in range(2):
                relay_copy(v, i).wait_send()
        for j in range(2):
            @pl.when(jnp.logical_not(own_quarter(j)))
            def _():
                res_copy(v, j).wait_send()
    for i in range(len(offsets)):
        rd_copy(i).wait_send()
    y_copy.wait_send()


def per_chip(grid_points, mic_coords, wavenumbers, pressures):
    bins, parts, snaps, mics = pressures.shape
    rows = parts * snaps
    points = grid_points.shape[1]
    norm_scale = 1.0 / math.sqrt(points * lax.axis_size("grid"))
    vmem = pl.BlockSpec(memory_space=pltpu.VMEM)
    dma = pltpu.SemaphoreType.DMA
    blocks = 2 * points // BLOCK
    solution, residual = pl.pallas_call(
        functools.partial(kernel, norm_scale),
        out_shape=(jax.ShapeDtypeStruct((bins, rows, points), F32), jax.ShapeDtypeStruct((bins, rows, mics), F32)),
        in_specs=[pl.BlockSpec(memory_space=pltpu.HBM)] * 4,
        out_specs=(vmem, vmem),
        scratch_shapes=[
            pltpu.VMEM((2, 3, points), F32),
            pltpu.VMEM((2, 3, mics), F32),
            pltpu.VMEM((1, bins), F32),
            pltpu.VMEM((bins, rows, mics), F32),
            pltpu.VMEM((128, 2 * points), F32),
            pltpu.VMEM((32, 2 * mics), F32),
            pltpu.VMEM((2 * points, 128), BF16),
            pltpu.VMEM((128, 2 * mics), BF16),
            pltpu.VMEM((2 * points, 2 * mics), BF16),
            pltpu.VMEM((2 * points, 2 * mics), BF16),
            pltpu.VMEM((bins, rows, mics), BF16),
            pltpu.VMEM((2, rows, mics), BF16),
            pltpu.VMEM((rows, 2 * mics), BF16),
            pltpu.VMEM((rows, 2 * mics), BF16),
            pltpu.VMEM((2, rows, 2 * points), F32),
            pltpu.VMEM((2, rows, 2 * points), F32),
            pltpu.VMEM((2, rows, 2 * points), F32),
            pltpu.VMEM((2, rows, 2 * mics), F32),
            pltpu.VMEM((2, 2, rows, points), BF16),
            pltpu.VMEM((2, 2, rows, mics), BF16),
            pltpu.VMEM((2, bins, rows, points), BF16),
            pltpu.VMEM((2, bins, rows, mics), BF16),
            pltpu.VMEM((8, 128), F32),
            pltpu.VMEM((16, 8, 128), F32),
            pltpu.VMEM((8, 128), F32),
            pltpu.VMEM((8, 128), F32),
            dma((5,)), dma((4,)), dma((4,)), dma((2,)),
            dma((2, blocks)), dma((2, blocks)), dma((2, 4)), dma((2, 4)),
            dma((2, 2)), dma((2, 4)), dma((2, 4)), dma((15,)), dma((15,)), dma((2,)), dma((4,)), dma((2, 2)),
        ],
        compiler_params=pltpu.CompilerParams(
            collective_id=0, has_side_effects=True, vmem_limit_bytes=64 * 1024 * 1024 - 65536),
    )(grid_points, mic_coords, wavenumbers.reshape(1, bins), pressures.reshape(bins, rows, mics))
    return (solution.reshape(bins, parts, snaps, points), residual.reshape(pressures.shape))


ITERS = 2


def steering_tiles(grid_points, mic_coords, wavenumbers, norm_scale):
    dist_x = grid_points[0][:, None] - mic_coords[0][None, :]
    dist_y = grid_points[1][:, None] - mic_coords[1][None, :]
    dist_z = grid_points[2][:, None] - mic_coords[2][None, :]
    radius = jnp.sqrt(dist_x * dist_x + dist_y * dist_y + dist_z * dist_z)
    amplitude = norm_scale / radius
    cos_list = []
    sin_list = []
    for bin_index in range(wavenumbers.shape[0]):
        phase_angle = wavenumbers[bin_index] * radius
        cos_list.append((jnp.cos(phase_angle) * amplitude).astype(jnp.bfloat16))
        sin_list.append((jnp.sin(phase_angle) * amplitude).astype(jnp.bfloat16))
    return (jnp.stack(cos_list), jnp.stack(sin_list))


def body(grid_points, mic_coords, wavenumbers, pressures):
    bin_count = pressures.shape[0]
    snap_count = pressures.shape[2]
    grid_local = grid_points.shape[1]
    norm_scale = 1.0 / math.sqrt(grid_local * lax.axis_size("grid"))
    cos_tiles, sin_tiles = steering_tiles(grid_points, mic_coords, wavenumbers, norm_scale)

    def combine_adjoint(cos_sum, sin_sum):
        real_part = cos_sum[:, :snap_count] - sin_sum[:, snap_count:]
        imag_part = cos_sum[:, snap_count:] + sin_sum[:, :snap_count]
        return jnp.stack([real_part, imag_part], axis=1)

    def apply_adjoint(residual):
        rounded = residual.astype(jnp.bfloat16).reshape(
            bin_count, 2 * snap_count, residual.shape[3]
        )
        cos_sum = jnp.einsum("fkm,fgm->fkg", rounded, cos_tiles, preferred_element_type=jnp.float32)
        sin_sum = jnp.einsum("fkm,fgm->fkg", rounded, sin_tiles, preferred_element_type=jnp.float32)
        partial_terms = combine_adjoint(cos_sum, sin_sum)
        summed = lax.psum(partial_terms, "mic")
        grad_norm = lax.psum(jnp.sum(summed * summed), ("grid", "bin"))
        return (summed, grad_norm)

    residual = pressures
    gradient, grad_norm = apply_adjoint(residual)
    direction = gradient
    solution = jnp.zeros_like(gradient)
    for iteration in range(ITERS):
        apply_rounded = direction.astype(jnp.bfloat16).reshape(
            bin_count, 2 * snap_count, direction.shape[3]
        )
        apply_cos_sum = jnp.einsum(
            "fkg,fgm->fkm", apply_rounded, cos_tiles, preferred_element_type=jnp.float32
        )
        apply_sin_sum = jnp.einsum(
            "fkg,fgm->fkm", apply_rounded, sin_tiles, preferred_element_type=jnp.float32
        )
        combine_real_part = apply_cos_sum[:, :snap_count] + apply_sin_sum[:, snap_count:]
        combine_imag_part = apply_cos_sum[:, snap_count:] - apply_sin_sum[:, :snap_count]
        apply_partial_terms = jnp.stack([combine_real_part, combine_imag_part], axis=1)
        apply_summed = lax.psum(apply_partial_terms, "grid")
        image_norm = lax.psum(jnp.sum(apply_summed * apply_summed), ("mic", "bin"))
        image, image_norm = (apply_summed, image_norm)
        step_size = grad_norm / image_norm
        solution = solution + step_size * direction
        residual = residual - step_size * image
        if iteration + 1 < ITERS:
            gradient, next_norm = apply_adjoint(residual)
            direction = gradient + next_norm / grad_norm * direction
            grad_norm = next_norm
    return (solution, residual)


def solution(mesh):
    placed = (P(None, "grid"), P(None, "mic"), P("bin"), P("bin", None, None, "mic"))
    sizes = (mesh.shape["grid"], mesh.shape["mic"], mesh.shape["bin"])
    return jax.shard_map(
        per_chip if sizes == (2, 4, 4) else body,
        mesh=mesh,
        in_specs=placed,
        out_specs=(P("bin", None, None, "grid"), P("bin", None, None, "mic")),
        check_vma=False,
    )
```

```python
import functools
import math

import jax
import jax.numpy as jnp
from jax import lax
from jax.experimental import pallas as pl
from jax.experimental.pallas import tpu as pltpu
from jax.sharding import PartitionSpec as P

MESH = pl.DeviceIdType.MESH
F32 = jnp.float32
BF16 = jnp.bfloat16

SIN_COEF = (4.4428679, -7.30744342, 3.59478804, -0.78437393)
COS_COEF = (1.41420408, -6.97764205, 5.71523831, -1.72834838)
ROUNDER = 12582912.0
ROWS = 256
TILE = 256
BLOCK = 512


def poly(coef, s):
    total = coef[-1]
    for value in coef[-2::-1]:
        total = total * s + value
    return total


def kernel(norm_scale, gp_ref, mc_ref, wn_ref, p_ref, sol_ref, res_ref,
           gp_all, mc_all, wn_buf, p_loc, g_rows, m_rows, g_mat, m_mat, cos_t, sin_t, p_send, p_all, op_a, op_b,
           part, part_in, grad, image, grad_half, image_half, sol_in, res_in,
           red_out, red_in, red_y, red_y_in,
           co_send, co_recv, p_ssem, p_rsem, ex_ssem, ex_rsem, so_ssem, so_rsem,
           re_ssem, re_rsem, fw_ssem, rd_ssem, rd_rsem, ry_sem, in_sem, rl_ssem):
    x, z, b = lax.axis_index("grid"), lax.axis_index("mic"), lax.axis_index("bin")
    y, c = b // 2, b % 2
    half = z // 2
    n_mic = mc_ref.shape[1]
    n_grid = gp_ref.shape[1]

    def dev(gx, mz, core, plane=None):
        plane = y if plane is None else plane
        return {"grid": gx, "mic": mz, "bin": plane * 2 + core}

    other_core = dev(x, z, 1 - c)

    def rcopy(src, dst, ssem, rsem, device):
        return pltpu.make_async_remote_copy(
            src_ref=src, dst_ref=dst, send_sem=ssem, recv_sem=rsem, device_id=device, device_id_type=MESH)

    offsets = [(dx, dz, dc) for dx in range(2) for dz in range(4) for dc in range(2)][1:]

    def at_offset(o):
        return dev((x + o[0]) % 2, (z + o[1]) % 4, (c + o[2]) % 2)

    barrier = pltpu.get_barrier_semaphore()
    for o in offsets:
        pl.semaphore_signal(barrier, inc=1, device_id=at_offset(o), device_id_type=MESH)
    pl.semaphore_signal(barrier, inc=1, device_id=dev(x, z, c, 1 - y), device_id_type=MESH)
    p_load = pltpu.make_async_copy(p_ref, p_loc, in_sem.at[0])
    p_load.start()
    gp_load = pltpu.make_async_copy(gp_ref, gp_all.at[x], in_sem.at[1])
    gp_load.start()
    mc_load = pltpu.make_async_copy(mc_ref, mc_all.at[z % 2], in_sem.at[2])
    wn_load = pltpu.make_async_copy(wn_ref, wn_buf, in_sem.at[3])

    @pl.when(c == half)
    def _():
        mc_load.start()

    @pl.when(c == x)
    def _():
        wn_load.start()

    g_rows[...] = jnp.zeros(g_rows.shape, F32)
    m_rows[...] = jnp.zeros(m_rows.shape, F32)
    m_mat[...] = jnp.zeros(m_mat.shape, BF16)
    pl.semaphore_wait(barrier, len(offsets) + 1)

    gp_copy = rcopy(gp_ref, gp_all.at[x], co_send.at[0], co_recv.at[0], dev(1 - x, z, c))
    gp_copy.start()

    def mic_copy(shift):
        return rcopy(mc_ref, mc_all.at[z % 2], co_send.at[1 + shift], co_recv.at[1 + z % 2],
                     dev(x, (z + shift) % 4, c))

    @pl.when(c == half)
    def _():
        for shift in range(1, 4):
            mic_copy(shift).start()

    wn_copy = rcopy(wn_ref, wn_buf, co_send.at[0 + 4], co_recv.at[3], other_core)

    @pl.when(c == x)
    def _():
        wn_copy.start()

    def p_copy(shift):
        to = (z + shift) % 4
        return rcopy(p_send.at[to], p_all.at[z % 2], p_ssem.at[shift], p_rsem.at[z % 2], dev(x, to, half))

    p_load.wait()

    @pl.when(c == x)
    def _():
        p_send[...] = p_loc[...].astype(BF16)
        for shift in range(4):
            if shift:
                p_copy(shift).start()
            else:
                @pl.when(c != half)
                def _():
                    p_copy(0).start()

                @pl.when(c == half)
                def _():
                    p_all[z % 2] = p_send[z]

    gp_load.wait()

    @pl.when(c == half)
    def _():
        mc_load.wait()

    @pl.when(c == x)
    def _():
        wn_load.wait()

    gp_copy.wait_recv()
    for j in range(2):
        @pl.when(z != 2 * c + j)
        def _():
            rcopy(mc_ref, mc_all.at[j], co_send.at[1], co_recv.at[1 + j], other_core).wait_recv()

    @pl.when(c != x)
    def _():
        wn_copy.wait_recv()

    here = lax.broadcasted_iota(jnp.int32, wn_buf.shape, 1) == z
    wavenumber = jnp.sum(jnp.where(here, wn_buf[...], 0.0), axis=1, keepdims=True)
    turns = wavenumber * (1.0 / (2.0 * math.pi))
    scale_row = jnp.broadcast_to(turns * norm_scale, (32, 128))

    def pieces(v):
        high = v.astype(BF16).astype(F32)
        rest = v - high
        mid = rest.astype(BF16).astype(F32)
        return high, mid, (rest - mid).astype(BF16).astype(F32)

    def fill(out, h, width, left, norm_at, one_at, v):
        cols = slice(h * width, (h + 1) * width)
        split = pieces(v)
        for i, which in enumerate(left):
            out[3 * i:3 * i + 3, cols] = split[which]
        for i, value in enumerate(pieces(jnp.sum(v * v, axis=0, keepdims=True))):
            out[norm_at + i:norm_at + i + 1, cols] = value
        out[one_at:one_at + 3, cols] = jnp.ones((3, width), F32)

    for h in range(2):
        fill(g_rows, h, n_grid, (0, 0, 1, 1, 0, 2), 18, 21, gp_all[h] * turns)
        fill(m_rows, h, n_mic, (0, 1, 0, 1, 2, 0), 21, 18, mc_all[h] * turns)
    row_index = lax.broadcasted_iota(jnp.int32, (32, 1), 0)
    m_mat[0:32, :] = (m_rows[...] * jnp.where(row_index < 18, -2.0, 1.0)).astype(BF16)
    for k in range(2 * n_grid // 128):
        g_mat[k * 128:(k + 1) * 128, :] = g_rows[:, k * 128:(k + 1) * 128].T.astype(BF16)

    @pl.loop(0, 2 * n_grid // ROWS)
    def _(i):
        base = pl.multiple_of(i * ROWS, ROWS)
        points = g_mat[pl.ds(base, ROWS), :]
        for n in range(2 * n_mic // TILE):
            squares = jnp.dot(points, m_mat[:, n * TILE:(n + 1) * TILE], preferred_element_type=F32)
            for r in range(ROWS // 32):
                for k in range(TILE // 128):
                    q = squares[r * 32:(r + 1) * 32, k * 128:(k + 1) * 128]
                    inv = lax.rsqrt(q)
                    t = q * inv
                    amp = inv * scale_row
                    f = t - ((t + ROUNDER) - ROUNDER)
                    s = f * f
                    sine = f * poly(SIN_COEF, s)
                    cosine = poly(COS_COEF, s)
                    scaled = sine * amp
                    rows = pl.ds(base + r * 32, 32)
                    cols = slice(n * TILE + k * 128, n * TILE + (k + 1) * 128)
                    cos_t[rows, cols] = (amp - scaled * sine).astype(BF16)
                    sin_t[rows, cols] = (scaled * cosine).astype(BF16)

    for j in range(2):
        @pl.when(jnp.logical_not(jnp.logical_and(z == 2 * c + j, c == x)))
        def _():
            rcopy(p_send.at[0], p_all.at[j], p_ssem.at[0], p_rsem.at[j], other_core).wait_recv()

    def operands(blocks, adjoint):
        for j in range(2):
            v = blocks[j]
            real, imag = v[:16], v[16:]
            swapped = [-imag, real] if adjoint else [imag, -real]
            cols = slice(j * v.shape[1], (j + 1) * v.shape[1])
            op_a[:, cols] = v
            op_b[:, cols] = jnp.concatenate(swapped, axis=0)

    def products(accs, pairs):
        out = []
        for acc, (left, right) in zip(accs, pairs):
            prod = left * right
            out.append(acc + jnp.sum(prod.reshape(4, 8, prod.shape[1]), axis=0))
        return out

    def ex_copy(v, k):
        cols = pl.ds(k * BLOCK, BLOCK)
        return rcopy(part.at[v, :, cols], part_in.at[v, :, cols], ex_ssem.at[v, k], ex_rsem.at[v, k], other_core)

    def adjoint(v):
        for k in range(2 * n_grid // BLOCK):
            rows = slice(k * BLOCK, (k + 1) * BLOCK)
            dims = (((1,), (1,)), ((), ()))
            part[v, :, rows] = (
                lax.dot_general(op_a[...], cos_t[rows, :], dims, preferred_element_type=F32)
                + lax.dot_general(op_b[...], sin_t[rows, :], dims, preferred_element_type=F32))
            ex_copy(v, k).start()
        for k in range(2 * n_grid // BLOCK):
            cols = slice(k * BLOCK, (k + 1) * BLOCK)
            ex_copy(v, k).wait_recv()
            total = part[v, :, cols] + part_in[v, :, cols]
            grad[v, :, cols] = total
            h, low = divmod(k * BLOCK, n_grid)
            grad_half[v, h, :, low:low + BLOCK] = total.astype(BF16)

    def forward(v):
        for k in range(2 * n_mic // BLOCK):
            cols = slice(k * BLOCK, (k + 1) * BLOCK)
            total = (jnp.dot(op_a[...], cos_t[:, cols], preferred_element_type=F32)
                     + jnp.dot(op_b[...], sin_t[:, cols], preferred_element_type=F32))
            image[v, :, cols] = total
            h, low = divmod(k * BLOCK, n_mic)
            image_half[v, h, :, low:low + BLOCK] = total.astype(BF16)

    def sol_copy(v, shift):
        to = z // 2 + shift
        return rcopy(grad_half.at[v, c], sol_in.at[v, z], so_ssem.at[v, shift], so_rsem.at[v, z], dev(c, to, x))

    def own_block(shift):
        return jnp.logical_and(z // 2 + shift == z, c == x)

    def send_sol(v):
        for shift in range(3):
            @pl.when(jnp.logical_not(own_block(shift)))
            def _():
                sol_copy(v, shift).start()

        @pl.when(c == x)
        def _():
            sol_in[v, z] = grad_half[v, c]

    relays = jnp.logical_or(z == 1, z == 2)

    def relay_copy(v, i):
        l = jnp.where(z == 2, i, 2 + i)
        return rcopy(sol_in.at[v, l], sol_in.at[v, l], rl_ssem.at[v, i], so_rsem.at[v, l],
                     dev(x, jnp.where(z == 2, 3, 0), c))

    def relay_sol(v):
        @pl.when(relays)
        def _():
            for i in range(2):
                relay_copy(v, i).wait_recv()
                relay_copy(v, i).start()

    def res_copy(v, j):
        return rcopy(image_half.at[v, j], res_in.at[v, z], re_ssem.at[v, j], re_rsem.at[v, z], dev(x, 2 * c + j, x))

    def own_quarter(j):
        return jnp.logical_and(z == 2 * c + j, c == x)

    def send_res(v):
        for j in range(2):
            @pl.when(jnp.logical_not(own_quarter(j)))
            def _():
                res_copy(v, j).start()

            @pl.when(own_quarter(j))
            def _():
                res_in[v, z] = image_half[v, j]

    def fw_copy(v, l):
        return rcopy(res_in.at[v, l], res_in.at[v, l], fw_ssem.at[v, l], re_rsem.at[v, l], dev(1 - x, z, c))

    def forward_res(v):
        @pl.when(c == x)
        def _():
            for l in range(4):
                @pl.when(jnp.logical_not(jnp.logical_and(z == l, c == half)))
                def _():
                    fw_copy(v, l).wait_recv()
                fw_copy(v, l).start()

    operands([p_all[0], p_all[1]], True)
    adjoint(0)
    send_sol(0)
    operands([grad_half[0, 0], grad_half[0, 1]], False)
    forward(0)
    send_res(0)
    operands([image_half[0, 0], image_half[0, 1]], True)
    adjoint(1)
    send_sol(1)
    relay_sol(0)
    operands([grad_half[1, 0], grad_half[1, 1]], False)
    forward(1)

    zero = jnp.zeros((8, 128), F32)
    accs = [zero] * 6
    for k in range(2 * n_grid // 128):
        cols = slice(k * 128, (k + 1) * 128)
        g, u = grad[0, :, cols], grad[1, :, cols]
        accs[:3] = products(accs[:3], [(g, g), (g, u), (u, u)])
    for k in range(2 * n_mic // 128):
        cols = slice(k * 128, (k + 1) * 128)
        q, w = image[0, :, cols], image[1, :, cols]
        accs[3:] = products(accs[3:], [(q, q), (q, w), (w, w)])
    for i in range(6):
        weight = 0.5 if i < 3 else 1.0
        red_out[i:i + 1, :] = weight * jnp.sum(accs[i], axis=0, keepdims=True)
    red_out[6:8, :] = jnp.zeros((2, 128), F32)

    me = (x * 4 + z) * 2 + c

    def rd_copy(i):
        return rcopy(red_out, red_in.at[me], rd_ssem.at[i], rd_rsem.at[i], at_offset(offsets[i]))

    for i in range(len(offsets)):
        rd_copy(i).start()
    send_res(1)
    forward_res(0)
    relay_sol(1)
    red_in[me] = red_out[...]
    for i in range(len(offsets)):
        rd_copy(i).wait_recv()
    total = red_in[0]
    for i in range(1, len(offsets) + 1):
        total = total + red_in[i]
    red_y[...] = total
    y_copy = rcopy(red_y, red_y_in, ry_sem.at[0], ry_sem.at[1], dev(x, z, c, 1 - y))
    y_copy.start()
    forward_res(1)
    y_copy.wait_recv()
    sums = jnp.sum(red_y[...] + red_y_in[...], axis=1, keepdims=True)
    gg, gu, uu, qq, qw, ww = [sums[i:i + 1, :] for i in range(6)]
    step0 = gg / qq
    next_norm = gg - 2.0 * step0 * gu + step0 * step0 * uu
    grown = 1.0 + next_norm / gg
    image_norm = grown * grown * qq - 2.0 * grown * step0 * qw + step0 * step0 * ww
    step1 = next_norm / image_norm
    first = step0 + step1 * grown
    second = -(step1 * step0)

    for l in range(4):
        for v in range(2):
            relayed = jnp.logical_and(relays, (z == 2) if l < 2 else (z == 1))

            @pl.when(jnp.logical_not(jnp.logical_or(relayed, jnp.logical_and(z == l, c == x))))
            def _():
                rcopy(grad_half.at[v, 0], sol_in.at[v, l], so_ssem.at[v, 0], so_rsem.at[v, l],
                      other_core).wait_recv()
        sol_ref[l] = first * sol_in[0, l].astype(F32) + second * sol_in[1, l].astype(F32)
    for l in range(4):
        @pl.when(c != x)
        def _():
            for v in range(2):
                fw_copy(v, l).wait_recv()
        res_ref[l] = p_loc[l] - (first * res_in[0, l].astype(F32) + second * res_in[1, l].astype(F32))

    gp_copy.wait_send()

    @pl.when(c == half)
    def _():
        for shift in range(1, 4):
            mic_copy(shift).wait_send()

    @pl.when(c == x)
    def _():
        wn_copy.wait_send()
        for shift in range(1, 4):
            p_copy(shift).wait_send()

        @pl.when(c != half)
        def _():
            p_copy(0).wait_send()
        for v in range(2):
            for l in range(4):
                fw_copy(v, l).wait_send()
    for v in range(2):
        for k in range(2 * n_grid // BLOCK):
            ex_copy(v, k).wait_send()
        for shift in range(3):
            @pl.when(jnp.logical_not(own_block(shift)))
            def _():
                sol_copy(v, shift).wait_send()

        @pl.when(relays)
        def _():
            for i in range(2):
                relay_copy(v, i).wait_send()
        for j in range(2):
            @pl.when(jnp.logical_not(own_quarter(j)))
            def _():
                res_copy(v, j).wait_send()
    for i in range(len(offsets)):
        rd_copy(i).wait_send()
    y_copy.wait_send()


def per_chip(grid_points, mic_coords, wavenumbers, pressures):
    bins, parts, snaps, mics = pressures.shape
    rows = parts * snaps
    points = grid_points.shape[1]
    norm_scale = 1.0 / math.sqrt(points * lax.axis_size("grid"))
    vmem = pl.BlockSpec(memory_space=pltpu.VMEM)
    dma = pltpu.SemaphoreType.DMA
    blocks = 2 * points // BLOCK
    solution, residual = pl.pallas_call(
        functools.partial(kernel, norm_scale),
        out_shape=(jax.ShapeDtypeStruct((bins, rows, points), F32), jax.ShapeDtypeStruct((bins, rows, mics), F32)),
        in_specs=[pl.BlockSpec(memory_space=pltpu.HBM)] * 4,
        out_specs=(vmem, vmem),
        scratch_shapes=[
            pltpu.VMEM((2, 3, points), F32),
            pltpu.VMEM((2, 3, mics), F32),
            pltpu.VMEM((1, bins), F32),
            pltpu.VMEM((bins, rows, mics), F32),
            pltpu.VMEM((128, 2 * points), F32),
            pltpu.VMEM((32, 2 * mics), F32),
            pltpu.VMEM((2 * points, 128), BF16),
            pltpu.VMEM((128, 2 * mics), BF16),
            pltpu.VMEM((2 * points, 2 * mics), BF16),
            pltpu.VMEM((2 * points, 2 * mics), BF16),
            pltpu.VMEM((bins, rows, mics), BF16),
            pltpu.VMEM((2, rows, mics), BF16),
            pltpu.VMEM((rows, 2 * mics), BF16),
            pltpu.VMEM((rows, 2 * mics), BF16),
            pltpu.VMEM((2, rows, 2 * points), F32),
            pltpu.VMEM((2, rows, 2 * points), F32),
            pltpu.VMEM((2, rows, 2 * points), F32),
            pltpu.VMEM((2, rows, 2 * mics), F32),
            pltpu.VMEM((2, 2, rows, points), BF16),
            pltpu.VMEM((2, 2, rows, mics), BF16),
            pltpu.VMEM((2, bins, rows, points), BF16),
            pltpu.VMEM((2, bins, rows, mics), BF16),
            pltpu.VMEM((8, 128), F32),
            pltpu.VMEM((16, 8, 128), F32),
            pltpu.VMEM((8, 128), F32),
            pltpu.VMEM((8, 128), F32),
            dma((5,)), dma((4,)), dma((4,)), dma((2,)),
            dma((2, blocks)), dma((2, blocks)), dma((2, 4)), dma((2, 4)),
            dma((2, 2)), dma((2, 4)), dma((2, 4)), dma((15,)), dma((15,)), dma((2,)), dma((4,)), dma((2, 2)),
        ],
        compiler_params=pltpu.CompilerParams(
            collective_id=0, has_side_effects=True, vmem_limit_bytes=64 * 1024 * 1024 - 65536),
    )(grid_points, mic_coords, wavenumbers.reshape(1, bins), pressures.reshape(bins, rows, mics))
    return (solution.reshape(bins, parts, snaps, points), residual.reshape(pressures.shape))


ITERS = 2


def steering_tiles(grid_points, mic_coords, wavenumbers, norm_scale):
    dist_x = grid_points[0][:, None] - mic_coords[0][None, :]
    dist_y = grid_points[1][:, None] - mic_coords[1][None, :]
    dist_z = grid_points[2][:, None] - mic_coords[2][None, :]
    radius = jnp.sqrt(dist_x * dist_x + dist_y * dist_y + dist_z * dist_z)
    amplitude = norm_scale / radius
    cos_list = []
    sin_list = []
    for bin_index in range(wavenumbers.shape[0]):
        phase_angle = wavenumbers[bin_index] * radius
        cos_list.append((jnp.cos(phase_angle) * amplitude).astype(jnp.bfloat16))
        sin_list.append((jnp.sin(phase_angle) * amplitude).astype(jnp.bfloat16))
    return (jnp.stack(cos_list), jnp.stack(sin_list))


def body(grid_points, mic_coords, wavenumbers, pressures):
    bin_count = pressures.shape[0]
    snap_count = pressures.shape[2]
    grid_local = grid_points.shape[1]
    norm_scale = 1.0 / math.sqrt(grid_local * lax.axis_size("grid"))
    cos_tiles, sin_tiles = steering_tiles(grid_points, mic_coords, wavenumbers, norm_scale)

    def combine_adjoint(cos_sum, sin_sum):
        real_part = cos_sum[:, :snap_count] - sin_sum[:, snap_count:]
        imag_part = cos_sum[:, snap_count:] + sin_sum[:, :snap_count]
        return jnp.stack([real_part, imag_part], axis=1)

    def apply_adjoint(residual):
        rounded = residual.astype(jnp.bfloat16).reshape(
            bin_count, 2 * snap_count, residual.shape[3]
        )
        cos_sum = jnp.einsum("fkm,fgm->fkg", rounded, cos_tiles, preferred_element_type=jnp.float32)
        sin_sum = jnp.einsum("fkm,fgm->fkg", rounded, sin_tiles, preferred_element_type=jnp.float32)
        partial_terms = combine_adjoint(cos_sum, sin_sum)
        summed = lax.psum(partial_terms, "mic")
        grad_norm = lax.psum(jnp.sum(summed * summed), ("grid", "bin"))
        return (summed, grad_norm)

    residual = pressures
    gradient, grad_norm = apply_adjoint(residual)
    direction = gradient
    solution = jnp.zeros_like(gradient)
    for iteration in range(ITERS):
        apply_rounded = direction.astype(jnp.bfloat16).reshape(
            bin_count, 2 * snap_count, direction.shape[3]
        )
        apply_cos_sum = jnp.einsum(
            "fkg,fgm->fkm", apply_rounded, cos_tiles, preferred_element_type=jnp.float32
        )
        apply_sin_sum = jnp.einsum(
            "fkg,fgm->fkm", apply_rounded, sin_tiles, preferred_element_type=jnp.float32
        )
        combine_real_part = apply_cos_sum[:, :snap_count] + apply_sin_sum[:, snap_count:]
        combine_imag_part = apply_cos_sum[:, snap_count:] - apply_sin_sum[:, :snap_count]
        apply_partial_terms = jnp.stack([combine_real_part, combine_imag_part], axis=1)
        apply_summed = lax.psum(apply_partial_terms, "grid")
        image_norm = lax.psum(jnp.sum(apply_summed * apply_summed), ("mic", "bin"))
        image, image_norm = (apply_summed, image_norm)
        step_size = grad_norm / image_norm
        solution = solution + step_size * direction
        residual = residual - step_size * image
        if iteration + 1 < ITERS:
            gradient, next_norm = apply_adjoint(residual)
            direction = gradient + next_norm / grad_norm * direction
            grad_norm = next_norm
    return (solution, residual)


def solution(mesh):
    placed = (P(None, "grid"), P(None, "mic"), P("bin"), P("bin", None, None, "mic"))
    sizes = (mesh.shape["grid"], mesh.shape["mic"], mesh.shape["bin"])
    return jax.shard_map(
        per_chip if sizes == (2, 4, 4) else body,
        mesh=mesh,
        in_specs=placed,
        out_specs=(P("bin", None, None, "grid"), P("bin", None, None, "mic")),
        check_vma=False,
    )
```
